32 devices in a mesh: span: 8 (over z, x), cross: 4 (over y, core).
Axes of the slice: x: 2, y: 2, z: 4, core: 2. Of those that a mesh axis runs over, the one named last changes fastest.
Arguments:
- velocity: float32 [3, 512, 16, 128], P(None, 'span', 'cross'), may hold values from -6 to 6
- viscosity: float32 [512, 16, 128], P('span', 'cross'), may hold values from 0.02 to 0.4
Outputs:
- advanced: float32 [3, 512, 16, 128], P(None, 'span', 'cross')
The draws below stay inside these ranges and needn't reach their ends.
All inputs are finite; a program needn't handle non-finite values.
Results may differ from the reference program's by a relative error of at most 0.0001.
Values sent between devices are 32-bit elements; how exact they have to be, the bound alone decides.
A program may use at most 64 MiB of HBM per device.

```python
import math
import jax
import jax.numpy as jnp

NX = 128
SWEEPS = 4
NZ = 512
NY = 16


def steps_of(stream_key, shape, cuts, low, high):
    def one(axis_at, parts):
        steps = jax.random.uniform(jax.random.fold_in(jax.random.fold_in(stream_key, 6), axis_at), (parts,), jnp.float32, low / len(cuts), high / len(cuts))
        return jnp.repeat(jnp.exp(steps), shape[axis_at] // parts).reshape((-1,) + (1,) * (len(shape) - axis_at - 1))

    gain = one(*cuts[0])
    for cut in cuts[1:]:
        gain = gain * one(*cut)
    return gain


def gaussian(key, extent, scale, limit, shards=(), kind=jnp.bfloat16):
    array = jax.random.normal(key, extent, jnp.float32) * scale
    if len(shards) > 0:
        array = steps_of(key, extent, shards, -0.22, 0.18) * array
    return jnp.clip(array, min=-limit, max=limit).astype(kind)


def setup_inputs(seed: int = 0) -> dict:
    key_list = jax.random.split(jax.random.key(seed), 3)
    velocity = gaussian(key_list[0], (3, NZ, NY, NX), 1.0, 6.0, ((1, 8), (2, 4)), jnp.float32)
    viscosity = jnp.clip(jnp.exp(math.log(0.4) - 2.9957323 * jax.random.uniform(key_list[1], (NZ, NY, NX), jnp.float32) ** steps_of(key_list[1], (NZ, NY, NX), ((0, 8), (1, 4)), -0.2, 0.2)), 0.02, 0.4)
    return {"velocity": velocity, "viscosity": viscosity}


time_step = 0.1


def first_wave(number, length):
    angles = number * (2.0 * math.pi / length)
    return (14.0 / 9.0 * jnp.sin(angles) + 1.0 / 18.0 * jnp.sin(2.0 * angles)) / (1.0 + 2.0 / 3.0 * jnp.cos(angles))


def second_wave(number, length):
    angles = number * (2.0 * math.pi / length)
    return (24.0 / 11.0 * (1.0 - jnp.cos(angles)) + 3.0 / 22.0 * (1.0 - jnp.cos(2.0 * angles))) / (1.0 + 4.0 / 11.0 * jnp.cos(angles))


def stream_first(values):
    up_one = jnp.roll(values, -1, axis=-1)
    down_one = jnp.roll(values, 1, axis=-1)
    up_two = jnp.roll(values, -2, axis=-1)
    down_two = jnp.roll(values, 2, axis=-1)
    return (8.0 * (up_one - down_one) - (up_two - down_two)) / 12.0


def stream_curve(values):
    up_one = jnp.roll(values, -1, axis=-1)
    down_one = jnp.roll(values, 1, axis=-1)
    up_two = jnp.roll(values, -2, axis=-1)
    down_two = jnp.roll(values, 2, axis=-1)
    return (16.0 * (up_one + down_one) - (up_two + down_two) - 30.0 * values) / 12.0


def cross_pad(values):
    return jnp.pad(values, ((0, 0), (2, 2), (0, 0)))


def cross_slope(padded):
    return (8.0 * (padded[..., 3:-1, :] - padded[..., 1:-3, :]) - (padded[..., 4:, :] - padded[..., :-4, :])) / 12.0


def cross_curve(padded):
    return (16.0 * (padded[..., 3:-1, :] + padded[..., 1:-3, :]) - (padded[..., 4:, :] + padded[..., :-4, :]) - 30.0 * padded[..., 2:-2, :]) / 12.0


def span_pair(values):
    spectrum = jnp.fft.rfft(values, axis=0)
    number = jnp.arange(NZ // 2 + 1).astype(jnp.float32)[:, None, None]
    first_slope = jnp.fft.irfft(1j * first_wave(number, NZ) * spectrum, n=NZ, axis=0).astype(jnp.float32)
    second_slope = jnp.fft.irfft(-second_wave(number, NZ) * spectrum, n=NZ, axis=0).astype(jnp.float32)
    return first_slope, second_slope


def tendency(velocity, viscosity):
    results = []
    for component in range(3):
        values = velocity[component]
        padded = cross_pad(values)
        slope_z, curve_z = span_pair(values)
        carried = velocity[0] * stream_first(values) + velocity[1] * cross_slope(padded) + velocity[2] * slope_z
        results.append(viscosity * (stream_curve(values) + cross_curve(padded) + curve_z) - carried)
    return jnp.stack(results)


def project(section):
    joined = stream_first(section[0]) + cross_slope(cross_pad(section[1]))
    number = jnp.arange(NZ // 2 + 1).astype(jnp.float32)[:, None, None]
    source = jnp.fft.rfft(joined, axis=0) + 1j * first_wave(number, NZ) * jnp.fft.rfft(section[2], axis=0)
    diagonal = 4.0 + second_wave(number, NZ)
    potential = -source / diagonal
    for sweep_index in range(SWEEPS - 1):
        padded = jnp.pad(potential, ((0, 0), (1, 1), (0, 0)))
        beside_all = jnp.roll(potential, 1, axis=2) + jnp.roll(potential, -1, axis=2) + padded[:, 2:] + padded[:, :-2]
        potential = (beside_all - source) / diagonal
    scalar = jnp.fft.irfft(potential, n=NZ, axis=0).astype(jnp.float32)
    span_grad = jnp.fft.irfft(1j * first_wave(number, NZ) * potential, n=NZ, axis=0).astype(jnp.float32)
    return section - jnp.stack([stream_first(scalar), cross_slope(cross_pad(scalar)), span_grad])


def reference(velocity, viscosity):
    section_one = velocity + time_step * tendency(velocity, viscosity)
    first_pass = project(section_one)
    section_two = 0.5 * velocity + 0.5 * (first_pass + time_step * tendency(first_pass, viscosity))
    return project(section_two)
```

```python
import jax
import jax.numpy as jnp
import numpy as np
from jax import lax
from jax.experimental import pallas as pl
from jax.experimental.pallas import tpu as pltpu
from jax.sharding import PartitionSpec as P

MESH = pl.DeviceIdType.MESH
TIME_STEP = 0.1
FAR = 5
highest = lax.Precision.HIGHEST


def symbols(length):
    w = 2.0 * np.pi * np.arange(length) / length
    k1 = (14 / 9 * np.sin(w) + 1 / 18 * np.sin(2 * w)) / (1 + 2 / 3 * np.cos(w))
    k2 = (24 / 11 * (1 - np.cos(w)) + 3 / 22 * (1 - np.cos(2 * w))) / (1 + 4 / 11 * np.cos(w))
    return k1, k2


def block_form(table, cells, rank):
    length = table[0].shape[0]
    kernels = [np.fft.ifft(symbol).real for symbol in table]
    offset = np.arange(cells)[:, None] - np.arange(cells)[None, :]
    own = np.concatenate([h[offset % length] for h in kernels])
    left = np.concatenate([h[(offset + cells) % length] for h in kernels])
    right = np.concatenate([h[(offset - cells) % length] for h in kernels])
    to_right = np.linalg.svd(left)[2][:rank]
    to_left = np.linalg.svd(right)[2][:rank]
    sums = np.concatenate([to_right, to_left])
    apply = np.concatenate([own, left @ to_right.T, right @ to_left.T], axis=1)
    return sums.astype(np.float32), apply.astype(np.float32)


def turn(values, shift):
    axis = values.ndim - 1
    return pltpu.roll(values, shift % values.shape[axis], axis)


def wide(values):
    return jnp.concatenate([values[i] for i in range(values.shape[0])], axis=-1)


def tall(values, count):
    n = values.shape[-1] // count
    return jnp.stack([values[:, i * n:(i + 1) * n] for i in range(count)])


def stream_pair(values):
    up_one, down_one = turn(values, -1), turn(values, 1)
    up_two, down_two = turn(values, -2), turn(values, 2)
    first = (8.0 * (up_one - down_one) - (up_two - down_two)) * (1.0 / 12.0)
    curve = (16.0 * (up_one + down_one) - (up_two + down_two) - 30.0 * values) * (1.0 / 12.0)
    return first, curve


def stream_first(values):
    return (8.0 * (turn(values, -1) - turn(values, 1)) - (turn(values, -2) - turn(values, 2))) * (1.0 / 12.0)


def cross_slope(p):
    n = p.shape[0]
    return (8.0 * (p[3:n - 1] - p[1:n - 3]) - (p[4:] - p[:n - 4])) * (1.0 / 12.0)


def cross_curve(p):
    n = p.shape[0]
    return (16.0 * (p[3:n - 1] + p[1:n - 3]) - (p[4:] + p[:n - 4]) - 30.0 * p[2:n - 2]) * (1.0 / 12.0)


def beside(p):
    mid = p[1:p.shape[0] - 1]
    return turn(mid, 1) + turn(mid, -1) + p[2:] + p[:p.shape[0] - 2]


def kernel(spans, crosses, vel, visc, sums_a, form_a, sums_c, form_c, out,
           vx, za, zao, sx, zb, zbo, cx, zc, zco, send_sem, recv_sem):
    a, c = lax.axis_index("span"), lax.axis_index("cross")
    rows, cells = vel.shape[1], vel.shape[2]
    ra = sums_a.shape[0] // 2
    rc = sums_c.shape[0] // 2

    def device(da, dc):
        return lax.rem(a + (da + spans), spans), lax.rem(c + (dc + crosses), crosses)

    barrier = pltpu.get_barrier_semaphore()
    greeted = [(da, dc) for da in (-1, 0, 1) for dc in (-2, -1, 0, 1, 2) if (da, dc) != (0, 0)]
    for da, dc in greeted:
        pl.semaphore_signal(barrier, inc=1, device_id=device(da, dc), device_id_type=MESH)
    pl.semaphore_wait(barrier, len(greeted))

    def send(number, section, src, dst, da, dc):
        copy = pltpu.make_async_remote_copy(
            src_ref=src, dst_ref=dst, send_sem=send_sem.at[section, number],
            recv_sem=recv_sem.at[section, number], device_id=device(da, dc), device_id_type=MESH,
        )
        copy.start()
        return copy

    def inside(values, first):
        number = c * rows + first + lax.broadcasted_iota(jnp.int32, values.shape, 0)
        return jnp.where((number >= 0) & (number < rows * crosses), values, 0.0)

    def dot(left, right):
        return jnp.dot(left, right, precision=highest, preferred_element_type=jnp.float32)

    kept = []
    for t in range(2):
        copies = [
            send(0, t, vx.at[t, :, rows:rows + 2], vx.at[t, :, 0:2], 0, 1),
            send(1, t, vx.at[t, :, 2:4], vx.at[t, :, rows + 2:rows + 4], 0, -1),
        ] if t else []
        if not t:
            vx[t, :, 2:rows + 2] = vel[...]
            copies = [
                send(0, t, vx.at[t, :, rows:rows + 2], vx.at[t, :, 0:2], 0, 1),
                send(1, t, vx.at[t, :, 2:4], vx.at[t, :, rows + 2:rows + 4], 0, -1),
            ]
        base = vx[t, :, 2:rows + 2]
        flat = wide(base.reshape(3 * rows, cells, base.shape[-1]))
        edge = dot(sums_a[...], flat)
        zao[t, 0] = tall(edge[:ra], 3 * rows)
        zao[t, 1] = tall(edge[ra:], 3 * rows)
        copies += [
            send(2, t, zao.at[t, 0], za.at[t, 0], 1, 0),
            send(3, t, zao.at[t, 1], za.at[t, 1], -1, 0),
        ]
        local = dot(form_a[:, :cells], flat)
        slope_x, curve_x = stream_pair(base.reshape(3 * rows, cells, base.shape[-1]))
        for copy in copies:
            copy.wait_recv()
        kept += copies
        met = jnp.concatenate([wide(za[t, 0]), wide(za[t, 1])], axis=0)
        pair = local + dot(form_a[:, cells:], met)
        slope_z = tall(pair[:cells], 3 * rows)
        curve_z = tall(pair[cells:], 3 * rows)
        section = []
        nu = visc[...]
        for k in range(3):
            padded = inside(vx[t, k], -2)
            at = slice(k * rows, (k + 1) * rows)
            rate = nu * (curve_x[at] + cross_curve(padded) + curve_z[at]) - (
                base[0] * slope_x[at] + base[1] * cross_slope(padded) + base[2] * slope_z[at])
            if t:
                section.append(0.5 * vel[k] + 0.5 * (base[k] + TIME_STEP * rate))
            else:
                section.append(base[k] + TIME_STEP * rate)
        sx[t, 2:rows + 2] = section[1]
        copies = [
            send(4, t, sx.at[t, rows:rows + 2], sx.at[t, 0:2], 0, 1),
            send(5, t, sx.at[t, 2:4], sx.at[t, rows + 2:rows + 4], 0, -1),
        ]
        flat = wide(section[2])
        edge = dot(sums_a[...], flat)
        zbo[t, 0] = tall(edge[:ra], rows)
        zbo[t, 1] = tall(edge[ra:], rows)
        copies += [
            send(6, t, zbo.at[t, 0], zb.at[t, 0], 1, 0),
            send(7, t, zbo.at[t, 1], zb.at[t, 1], -1, 0),
        ]
        local = dot(form_a[:cells, :cells], flat)
        joined = stream_first(section[0])
        for copy in copies:
            copy.wait_recv()
        kept += copies
        met = jnp.concatenate([wide(zb[t, 0]), wide(zb[t, 1])], axis=0)
        source = joined + cross_slope(inside(sx[t], -2)) + tall(local + dot(form_a[:cells, cells:], met), rows)
        low, high = FAR, FAR + rows
        cx[t, low:high] = source
        copies = [
            send(8, t, cx.at[t, low:high], cx.at[t, low - rows:low], 0, 1),
            send(9, t, cx.at[t, low:high], cx.at[t, high:high + rows], 0, -1),
            send(10, t, cx.at[t, high - 1:high], cx.at[t, 0:1], 0, 2),
            send(11, t, cx.at[t, low:low + 1], cx.at[t, high + rows:high + rows + 1], 0, -2),
        ]
        edge = dot(sums_c[...], wide(source))
        number = 12
        for side in range(2):
            zco[t, side] = tall(edge[side * rc:(side + 1) * rc], rows)
            da = 1 - 2 * side
            copies += [
                send(number, t, zco.at[t, side], zc.at[t, side, low:high], da, 0),
                send(number + 1, t, zco.at[t, side], zc.at[t, side, low - rows:low], da, 1),
                send(number + 2, t, zco.at[t, side], zc.at[t, side, high:high + rows], da, -1),
                send(number + 3, t, zco.at[t, side, rows - 1:rows], zc.at[t, side, 0:1], da, 2),
                send(number + 4, t, zco.at[t, side, 0:1], zc.at[t, side, high + rows:high + rows + 1], da, -2),
            ]
            number += 5
        for copy in copies:
            copy.wait_recv()
        kept += copies
        total = rows + 2 * FAR
        joint = jnp.concatenate([cx[t], zc[t, 0], zc[t, 1]], axis=1)
        joint = inside(joint, -FAR)
        powers = dot(form_c[:4 * cells], wide(joint))
        slopes = dot(form_c[4 * cells:], wide(joint[2:total - 2]))
        t0, t1, t2, t3 = [tall(powers[i * cells:(i + 1) * cells], total) for i in range(4)]
        d0, d1, d2, d3 = [tall(slopes[i * cells:(i + 1) * cells], total - 4) for i in range(4)]
        x = inside(t2[1:total - 1] + beside(t3), 1 - FAR)
        x = inside(t1[2:total - 2] + beside(x), 2 - FAR)
        scalar = inside(t0[3:total - 3] + beside(x), 3 - FAR)
        n = total - 4
        x = inside(d2[1:n - 1] + beside(d3), 3 - FAR)
        x = inside(d1[2:n - 2] + beside(x), 4 - FAR)
        slope = d0[3:n - 3] + beside(x)
        results = [
            section[0] + stream_first(scalar[2:rows + 2]),
            section[1] + cross_slope(scalar),
            section[2] + slope,
        ]
        for k in range(3):
            if t:
                out[k] = results[k]
            else:
                vx[1, k, 2:rows + 2] = results[k]
    for copy in kept:
        copy.wait_send()


def solution(mesh):
    spans, crosses = mesh.shape["span"], mesh.shape["cross"]

    def per_device(velocity, viscosity):
        _, cells, rows, columns = velocity.shape
        k1, k2 = symbols(cells * spans)
        g = 1.0 / (4.0 + k2)
        sums_a, form_a = block_form([1j * k1, -k2 + 0j], cells, 8)
        powers = [g ** (m + 1) + 0j for m in range(4)]
        sums_c, form_c = block_form(powers + [1j * k1 * p for p in powers], cells, 16)
        total = rows + 2 * FAR
        f32 = jnp.float32
        vmem = pl.BlockSpec(memory_space=pltpu.VMEM)
        result = pl.pallas_call(
            lambda *refs: kernel(spans, crosses, *refs),
            out_shape=jax.ShapeDtypeStruct((3, rows, cells, columns), f32),
            in_specs=[vmem] * 6,
            out_specs=vmem,
            scratch_shapes=[
                pltpu.VMEM((2, 3, rows + 4, cells, columns), f32),
                pltpu.VMEM((2, 2, 3 * rows, 8, columns), f32),
                pltpu.VMEM((2, 2, 3 * rows, 8, columns), f32),
                pltpu.VMEM((2, rows + 4, cells, columns), f32),
                pltpu.VMEM((2, 2, rows, 8, columns), f32),
                pltpu.VMEM((2, 2, rows, 8, columns), f32),
                pltpu.VMEM((2, total, cells, columns), f32),
                pltpu.VMEM((2, 2, total, 16, columns), f32),
                pltpu.VMEM((2, 2, rows, 16, columns), f32),
                pltpu.SemaphoreType.DMA((2, 22)),
                pltpu.SemaphoreType.DMA((2, 22)),
            ],
            compiler_params=pltpu.CompilerParams(
                collective_id=0, has_side_effects=True, vmem_limit_bytes=40 * 1024 * 1024
            ),
        )(
            velocity.transpose(0, 2, 1, 3), viscosity.transpose(1, 0, 2),
            jnp.asarray(sums_a), jnp.asarray(form_a), jnp.asarray(sums_c), jnp.asarray(form_c),
        )
        return result.transpose(0, 2, 1, 3)

    return jax.shard_map(
        per_device,
        mesh=mesh,
        in_specs=(P(None, "span", "cross", None), P("span", "cross", None)),
        out_specs=P(None, "span", "cross", None),
        check_vma=False,
    )
```

```python
import jax
import jax.numpy as jnp
import numpy as np
from jax import lax
from jax.experimental import pallas as pl
from jax.experimental.pallas import tpu as pltpu
from jax.sharding import PartitionSpec as P

MESH = pl.DeviceIdType.MESH
TIME_STEP = 0.1
FAR = 5
RANK = 8


def symbols(length):
    w = 2.0 * np.pi * np.arange(length) / length
    k1 = (14 / 9 * np.sin(w) + 1 / 18 * np.sin(2 * w)) / (1 + 2 / 3 * np.cos(w))
    k2 = (24 / 11 * (1 - np.cos(w)) + 3 / 22 * (1 - np.cos(2 * w))) / (1 + 4 / 11 * np.cos(w))
    return k1, k2


def triple(table):
    high = table.astype(jnp.bfloat16)
    low = (table - high.astype(np.float64)).astype(jnp.bfloat16)
    return np.concatenate([high, low, high], axis=1).astype(np.float32)


def parts(values):
    high = values.astype(jnp.bfloat16)
    low = (values - high.astype(jnp.float32)).astype(jnp.bfloat16)
    return jnp.concatenate([high, high, low], axis=0)


def block_form(table, cells, rank):
    length = table[0].shape[0]
    kernels = [np.fft.ifft(symbol).real for symbol in table]
    offset = np.arange(cells)[:, None] - np.arange(cells)[None, :]
    own = np.concatenate([h[offset % length] for h in kernels])
    left = np.concatenate([h[(offset + cells) % length] for h in kernels])
    right = np.concatenate([h[(offset - cells) % length] for h in kernels])
    to_right = np.linalg.svd(left)[2][:rank]
    to_left = np.linalg.svd(right)[2][:rank]
    sums = np.concatenate([to_right, to_left])
    apply = np.concatenate([own, left @ to_right.T, right @ to_left.T], axis=1)
    return triple(sums), triple(apply)


def turn(values, shift):
    axis = values.ndim - 1
    return pltpu.roll(values, shift % values.shape[axis], axis)


def wide(values):
    return jnp.concatenate([values[i] for i in range(values.shape[0])], axis=-1)


def tall(values, count):
    n = values.shape[-1] // count
    return jnp.stack([values[:, i * n:(i + 1) * n] for i in range(count)])


def stream_pair(values):
    up_one, down_one = turn(values, -1), turn(values, 1)
    up_two, down_two = turn(values, -2), turn(values, 2)
    first = (8.0 * (up_one - down_one) - (up_two - down_two)) * (1.0 / 12.0)
    curve = (16.0 * (up_one + down_one) - (up_two + down_two) - 30.0 * values) * (1.0 / 12.0)
    return first, curve


def stream_first(values):
    return (8.0 * (turn(values, -1) - turn(values, 1)) - (turn(values, -2) - turn(values, 2))) * (1.0 / 12.0)


def cross_slope(p):
    n = p.shape[0]
    return (8.0 * (p[3:n - 1] - p[1:n - 3]) - (p[4:] - p[:n - 4])) * (1.0 / 12.0)


def cross_curve(p):
    n = p.shape[0]
    return (16.0 * (p[3:n - 1] + p[1:n - 3]) - (p[4:] + p[:n - 4]) - 30.0 * p[2:n - 2]) * (1.0 / 12.0)


def beside(p):
    mid = p[1:p.shape[0] - 1]
    return turn(mid, 1) + turn(mid, -1) + p[2:] + p[:p.shape[0] - 2]


def kernel(spans, crosses, vel, visc, sums_a, form_a, sums_c, form_c, out,
           vx, za, zao, sx, zb, zbo, cx, zc, zco, nu_ref, send_sem, recv_sem):
    a, c = lax.axis_index("span"), lax.axis_index("cross")
    rows, cells = nu_ref.shape[0], nu_ref.shape[1]
    ra = sums_a.shape[0] // 2
    rc = sums_c.shape[0] // 2

    def device(da, dc):
        return lax.rem(a + (da + spans), spans), lax.rem(c + (dc + crosses), crosses)

    def there(dc, action):
        if dc == 0:
            action()
        else:
            pl.when((c + dc >= 0) & (c + dc < crosses))(action)

    def clear(dc, refs):
        def action():
            for ref in refs:
                ref[...] = jnp.zeros(ref.shape, ref.dtype)

        pl.when((c + dc < 0) | (c + dc >= crosses))(action)

    barrier = pltpu.get_barrier_semaphore()
    greeted = [(da, dc) for da in (-1, 0, 1) for dc in (-2, -1, 0, 1, 2) if (da, dc) != (0, 0)]
    for da, dc in greeted:
        pl.semaphore_signal(barrier, inc=1, device_id=device(da, dc), device_id_type=MESH)

    def send(number, section, src, dst, da, dc):
        copy = pltpu.make_async_remote_copy(
            src_ref=src, dst_ref=dst, send_sem=send_sem.at[section, number],
            recv_sem=recv_sem.at[section, number], device_id=device(da, dc), device_id_type=MESH,
        )
        there(dc, copy.start)
        return copy, dc

    def arrive(copies):
        for copy, dc in copies:
            there(-dc, copy.wait_recv)

    def inside(values, first):
        number = c * rows + first + lax.broadcasted_iota(jnp.int32, values.shape, 0)
        return jnp.where((number >= 0) & (number < rows * crosses), values, 0.0)

    def dot(left, right):
        return jnp.dot(left.astype(jnp.bfloat16), right, preferred_element_type=jnp.float32)

    low, high = FAR, FAR + rows
    total = rows + 2 * FAR
    clear(-1, [vx.at[:, :, 0:2], sx.at[:, 0:2], cx.at[:, low - rows:low], zc.at[:, :, low - rows:low]])
    clear(1, [vx.at[:, :, rows + 2:], sx.at[:, rows + 2:], cx.at[:, high:high + rows], zc.at[:, :, high:high + rows]])
    clear(-2, [cx.at[:, 0:1], zc.at[:, :, 0:1]])
    clear(2, [cx.at[:, total - 1:], zc.at[:, :, total - 1:]])
    for y in range(rows):
        own = pl.ds(y, cells, stride=rows)
        for k in range(3):
            vx[0, k, y + 2] = vel[k, own, :]
        nu_ref[y] = visc[own, :]

    kept = []
    for t in range(2):
        if not t:
            pl.semaphore_wait(barrier, len(greeted))
        copies = [
            send(0, t, vx.at[t, :, rows:rows + 2], vx.at[t, :, 0:2], 0, 1),
            send(1, t, vx.at[t, :, 2:4], vx.at[t, :, rows + 2:rows + 4], 0, -1),
        ]
        base = vx[t, :, 2:rows + 2]
        flat = wide(base.reshape(3 * rows, cells, base.shape[-1]))
        edge = dot(sums_a[...], parts(flat))
        zao[t, 0] = tall(edge[:ra], 3 * rows)
        zao[t, 1] = tall(edge[ra:], 3 * rows)
        copies += [
            send(2, t, zao.at[t, 0], za.at[t, 0], 1, 0),
            send(3, t, zao.at[t, 1], za.at[t, 1], -1, 0),
        ]
        slope_x, curve_x = stream_pair(base.reshape(3 * rows, cells, base.shape[-1]))
        arrive(copies)
        kept += copies
        met = jnp.concatenate([flat, wide(za[t, 0]), wide(za[t, 1])], axis=0)
        pair = dot(form_a[...], parts(met))
        slope_z = tall(pair[:cells], 3 * rows)
        curve_z = tall(pair[cells:], 3 * rows)
        section = []
        nu = nu_ref[...]
        for k in range(3):
            padded = vx[t, k]
            at = slice(k * rows, (k + 1) * rows)
            rate = nu * (curve_x[at] + cross_curve(padded) + curve_z[at]) - (
                base[0] * slope_x[at] + base[1] * cross_slope(padded) + base[2] * slope_z[at])
            if t:
                section.append(0.5 * vx[0, k, 2:rows + 2] + 0.5 * (base[k] + TIME_STEP * rate))
            else:
                section.append(base[k] + TIME_STEP * rate)
        sx[t, 2:rows + 2] = section[1]
        copies = [
            send(4, t, sx.at[t, rows:rows + 2], sx.at[t, 0:2], 0, 1),
            send(5, t, sx.at[t, 2:4], sx.at[t, rows + 2:rows + 4], 0, -1),
        ]
        flat = wide(section[2])
        edge = dot(sums_a[...], parts(flat))
        zbo[t, 0] = tall(edge[:ra], rows)
        zbo[t, 1] = tall(edge[ra:], rows)
        copies += [
            send(6, t, zbo.at[t, 0], zb.at[t, 0], 1, 0),
            send(7, t, zbo.at[t, 1], zb.at[t, 1], -1, 0),
        ]
        joined = stream_first(section[0])
        arrive(copies)
        kept += copies
        met = jnp.concatenate([flat, wide(zb[t, 0]), wide(zb[t, 1])], axis=0)
        source = joined + cross_slope(sx[t]) + tall(dot(form_a[:cells], parts(met)), rows)
        cx[t, low:high] = source
        copies = [
            send(8, t, cx.at[t, low:high], cx.at[t, low - rows:low], 0, 1),
            send(9, t, cx.at[t, low:high], cx.at[t, high:high + rows], 0, -1),
            send(10, t, cx.at[t, high - 1:high], cx.at[t, 0:1], 0, 2),
            send(11, t, cx.at[t, low:low + 1], cx.at[t, high + rows:high + rows + 1], 0, -2),
        ]
        edge = dot(sums_c[...], parts(wide(source)))
        number = 12
        for side in range(2):
            zco[t, side] = tall(edge[side * rc:(side + 1) * rc], rows)
            da = 1 - 2 * side
            copies += [
                send(number, t, zco.at[t, side], zc.at[t, side, low:high], da, 0),
                send(number + 1, t, zco.at[t, side], zc.at[t, side, low - rows:low], da, 1),
                send(number + 2, t, zco.at[t, side], zc.at[t, side, high:high + rows], da, -1),
                send(number + 3, t, zco.at[t, side, rows - 1:rows], zc.at[t, side, 0:1], da, 2),
                send(number + 4, t, zco.at[t, side, 0:1], zc.at[t, side, high + rows:high + rows + 1], da, -2),
            ]
            number += 5
        arrive(copies)
        kept += copies
        joint = jnp.concatenate([cx[t], zc[t, 0], zc[t, 1]], axis=1)
        columns = joint.shape[-1]
        joint = parts(wide(joint))
        powers = dot(form_c[:4 * cells], joint)
        slopes = dot(form_c[4 * cells:], joint[:, 2 * columns:(total - 2) * columns])
        t0, t1, t2, t3 = [tall(powers[i * cells:(i + 1) * cells], total) for i in range(4)]
        d0, d1, d2, d3 = [tall(slopes[i * cells:(i + 1) * cells], total - 4) for i in range(4)]
        x = inside(t2[1:total - 1] + beside(t3), 1 - FAR)
        x = inside(t1[2:total - 2] + beside(x), 2 - FAR)
        scalar = inside(t0[3:total - 3] + beside(x), 3 - FAR)
        n = total - 4
        x = inside(d2[1:n - 1] + beside(d3), 3 - FAR)
        x = inside(d1[2:n - 2] + beside(x), 4 - FAR)
        slope = d0[3:n - 3] + beside(x)
        results = [
            section[0] + stream_first(scalar[2:rows + 2]),
            section[1] + cross_slope(scalar),
            section[2] + slope,
        ]
        for k in range(3):
            if t:
                for y in range(rows):
                    out[k, pl.ds(y, cells, stride=rows), :] = results[k][y]
            else:
                vx[1, k, 2:rows + 2] = results[k]
    for copy, dc in kept:
        there(dc, copy.wait_send)


def solution(mesh):
    spans, crosses = mesh.shape["span"], mesh.shape["cross"]

    def per_device(velocity, viscosity):
        _, cells, rows, columns = velocity.shape
        k1, k2 = symbols(cells * spans)
        g = 1.0 / (4.0 + k2)
        sums_a, form_a = block_form([1j * k1, -k2 + 0j], cells, 8)
        powers = [g ** (m + 1) + 0j for m in range(4)]
        sums_c, form_c = block_form(powers + [1j * k1 * p for p in powers], cells, RANK)
        total = rows + 2 * FAR
        f32 = jnp.float32
        vmem = pl.BlockSpec(memory_space=pltpu.VMEM)
        result = pl.pallas_call(
            lambda *refs: kernel(spans, crosses, *refs),
            out_shape=jax.ShapeDtypeStruct((3, cells * rows, columns), f32),
            in_specs=[vmem] * 6,
            out_specs=vmem,
            scratch_shapes=[
                pltpu.VMEM((2, 3, rows + 4, cells, columns), f32),
                pltpu.VMEM((2, 2, 3 * rows, 8, columns), f32),
                pltpu.VMEM((2, 2, 3 * rows, 8, columns), f32),
                pltpu.VMEM((2, rows + 4, cells, columns), f32),
                pltpu.VMEM((2, 2, rows, 8, columns), f32),
                pltpu.VMEM((2, 2, rows, 8, columns), f32),
                pltpu.VMEM((2, total, cells, columns), f32),
                pltpu.VMEM((2, 2, total, RANK, columns), f32),
                pltpu.VMEM((2, 2, rows, RANK, columns), f32),
                pltpu.VMEM((rows, cells, columns), f32),
                pltpu.SemaphoreType.DMA((2, 22)),
                pltpu.SemaphoreType.DMA((2, 22)),
            ],
            compiler_params=pltpu.CompilerParams(
                collective_id=0, has_side_effects=True, vmem_limit_bytes=40 * 1024 * 1024
            ),
        )(
            velocity.reshape(3, cells * rows, columns), viscosity.reshape(cells * rows, columns),
            jnp.asarray(sums_a), jnp.asarray(form_a), jnp.asarray(sums_c), jnp.asarray(form_c),
        )
        return result.reshape(3, cells, rows, columns)

    return jax.shard_map(
        per_device,
        mesh=mesh,
        in_specs=(P(None, "span", "cross", None), P("span", "cross", None)),
        out_specs=P(None, "span", "cross", None),
        check_vma=False,
    )
```

```python
import jax
import jax.numpy as jnp
import numpy as np
from jax import lax
from jax.experimental import pallas as pl
from jax.experimental.pallas import tpu as pltpu
from jax.sharding import PartitionSpec as P

MESH = pl.DeviceIdType.MESH
TIME_STEP = 0.1
FAR = 5
RANK = 8


def symbols(length):
    w = 2.0 * np.pi * np.arange(length) / length
    k1 = (14 / 9 * np.sin(w) + 1 / 18 * np.sin(2 * w)) / (1 + 2 / 3 * np.cos(w))
    k2 = (24 / 11 * (1 - np.cos(w)) + 3 / 22 * (1 - np.cos(2 * w))) / (1 + 4 / 11 * np.cos(w))
    return k1, k2


def triple(table):
    high = table.astype(jnp.bfloat16)
    low = (table - high.astype(np.float64)).astype(jnp.bfloat16)
    return np.concatenate([high, low, high], axis=1).astype(np.float32)


def parts(values):
    high = values.astype(jnp.bfloat16)
    low = (values - high.astype(jnp.float32)).astype(jnp.bfloat16)
    return jnp.concatenate([high, high, low], axis=0)


def block_form(table, cells, rank):
    length = table[0].shape[0]
    kernels = [np.fft.ifft(symbol).real for symbol in table]
    offset = np.arange(cells)[:, None] - np.arange(cells)[None, :]
    own = np.concatenate([h[offset % length] for h in kernels])
    left = np.concatenate([h[(offset + cells) % length] for h in kernels])
    right = np.concatenate([h[(offset - cells) % length] for h in kernels])
    to_right = np.linalg.svd(left)[2][:rank]
    to_left = np.linalg.svd(right)[2][:rank]
    sums = np.concatenate([to_right, to_left])
    apply = np.concatenate([own, left @ to_right.T, right @ to_left.T], axis=1)
    return triple(sums), triple(apply)


def turn(values, shift):
    axis = values.ndim - 1
    return pltpu.roll(values, shift % values.shape[axis], axis)


def wide(values):
    return jnp.concatenate([values[i] for i in range(values.shape[0])], axis=-1)


def tall(values, count):
    n = values.shape[-1] // count
    return jnp.stack([values[:, i * n:(i + 1) * n] for i in range(count)])


def stream_pair(values):
    up_one, down_one = turn(values, -1), turn(values, 1)
    up_two, down_two = turn(values, -2), turn(values, 2)
    first = (8.0 * (up_one - down_one) - (up_two - down_two)) * (1.0 / 12.0)
    curve = (16.0 * (up_one + down_one) - (up_two + down_two) - 30.0 * values) * (1.0 / 12.0)
    return first, curve


def stream_first(values):
    return (8.0 * (turn(values, -1) - turn(values, 1)) - (turn(values, -2) - turn(values, 2))) * (1.0 / 12.0)


def cross_slope(p):
    n = p.shape[0]
    return (8.0 * (p[3:n - 1] - p[1:n - 3]) - (p[4:] - p[:n - 4])) * (1.0 / 12.0)


def cross_curve(p):
    n = p.shape[0]
    return (16.0 * (p[3:n - 1] + p[1:n - 3]) - (p[4:] + p[:n - 4]) - 30.0 * p[2:n - 2]) * (1.0 / 12.0)


def beside(p):
    mid = p[1:p.shape[0] - 1]
    return turn(mid, 1) + turn(mid, -1) + p[2:] + p[:p.shape[0] - 2]


def kernel(spans, crosses, vel_hbm, visc_hbm, table_hbm, out, vel, visc, table, load_sem,
           vx, za, zao, sx, zb, zbo, cx, zc, zco, nu_ref, send_sem, recv_sem):
    a, c = lax.axis_index("span"), lax.axis_index("cross")
    rows, cells = nu_ref.shape[0], nu_ref.shape[1]
    ra = rc = RANK
    loads = [
        pltpu.make_async_copy(source, target, load_sem.at[i])
        for i, (source, target) in enumerate([(vel_hbm, vel), (visc_hbm, visc), (table_hbm, table)])
    ]
    for load in loads:
        load.start()
    n_sums = 2 * RANK
    sums_a = table.at[0:n_sums]
    sums_c = table.at[n_sums:2 * n_sums]
    form_a = table.at[2 * n_sums:2 * n_sums + 2 * cells]
    form_c = table.at[2 * n_sums + 2 * cells:]

    def device(da, dc):
        return lax.rem(a + (da + spans), spans), lax.rem(c + (dc + crosses), crosses)

    def there(dc, action):
        if dc == 0:
            action()
        else:
            pl.when((c + dc >= 0) & (c + dc < crosses))(action)

    def clear(dc, refs):
        def action():
            for ref in refs:
                ref[...] = jnp.zeros(ref.shape, ref.dtype)

        pl.when((c + dc < 0) | (c + dc >= crosses))(action)

    barrier = pltpu.get_barrier_semaphore()
    greeted = [(da, dc) for da in (-1, 0, 1) for dc in (-2, -1, 0, 1, 2) if (da, dc) != (0, 0)]
    for da, dc in greeted:
        pl.semaphore_signal(barrier, inc=1, device_id=device(da, dc), device_id_type=MESH)

    def send(number, section, src, dst, da, dc):
        copy = pltpu.make_async_remote_copy(
            src_ref=src, dst_ref=dst, send_sem=send_sem.at[section, number],
            recv_sem=recv_sem.at[section, number], device_id=device(da, dc), device_id_type=MESH,
        )
        there(dc, copy.start)
        return copy, dc

    def arrive(copies):
        for copy, dc in copies:
            there(-dc, copy.wait_recv)

    def inside(values, first):
        number = c * rows + first + lax.broadcasted_iota(jnp.int32, values.shape, 0)
        return jnp.where((number >= 0) & (number < rows * crosses), values, 0.0)

    def dot(left, right):
        rest = jnp.zeros((left.shape[1] - right.shape[0], right.shape[1]), right.dtype)
        right = jnp.concatenate([right, rest], axis=0)
        return jnp.dot(left.astype(jnp.bfloat16), right, preferred_element_type=jnp.float32)

    low, high = FAR, FAR + rows
    total = rows + 2 * FAR
    clear(-1, [vx.at[:, :, 0:2], sx.at[:, 0:2], cx.at[:, low - rows:low], zc.at[:, :, low - rows:low]])
    clear(1, [vx.at[:, :, rows + 2:], sx.at[:, rows + 2:], cx.at[:, high:high + rows], zc.at[:, :, high:high + rows]])
    clear(-2, [cx.at[:, 0:1], zc.at[:, :, 0:1]])
    clear(2, [cx.at[:, total - 1:], zc.at[:, :, total - 1:]])
    for load in loads:
        load.wait()
    for y in range(rows):
        own = pl.ds(y, cells, stride=rows)
        for k in range(3):
            vx[0, k, y + 2] = vel[k, own, :]
        nu_ref[y] = visc[own, :]

    kept = []
    for t in range(2):
        if not t:
            pl.semaphore_wait(barrier, len(greeted))
        copies = [
            send(0, t, vx.at[t, :, rows:rows + 2], vx.at[t, :, 0:2], 0, 1),
            send(1, t, vx.at[t, :, 2:4], vx.at[t, :, rows + 2:rows + 4], 0, -1),
        ]
        base = vx[t, :, 2:rows + 2]
        flat = wide(base.reshape(3 * rows, cells, base.shape[-1]))
        edge = dot(sums_a[...], parts(flat))
        zao[t, 0] = tall(edge[:ra], 3 * rows)
        zao[t, 1] = tall(edge[ra:], 3 * rows)
        copies += [
            send(2, t, zao.at[t, 0], za.at[t, 0], 1, 0),
            send(3, t, zao.at[t, 1], za.at[t, 1], -1, 0),
        ]
        slope_x, curve_x = stream_pair(base.reshape(3 * rows, cells, base.shape[-1]))
        arrive(copies)
        kept += copies
        met = jnp.concatenate([flat, wide(za[t, 0]), wide(za[t, 1])], axis=0)
        pair = dot(form_a[...], parts(met))
        slope_z = tall(pair[:cells], 3 * rows)
        curve_z = tall(pair[cells:], 3 * rows)
        section = [None] * 3
        nu = nu_ref[...]
        copies = []
        for k in (2, 1, 0):
            padded = vx[t, k]
            at = slice(k * rows, (k + 1) * rows)
            rate = nu * (curve_x[at] + cross_curve(padded) + curve_z[at]) - (
                base[0] * slope_x[at] + base[1] * cross_slope(padded) + base[2] * slope_z[at])
            if t:
                section[k] = 0.5 * vx[0, k, 2:rows + 2] + 0.5 * (base[k] + TIME_STEP * rate)
            else:
                section[k] = base[k] + TIME_STEP * rate
            if k == 2:
                flat = wide(section[2])
                edge = dot(sums_a[...], parts(flat))
                zbo[t, 0] = tall(edge[:ra], rows)
                zbo[t, 1] = tall(edge[ra:], rows)
                copies += [
                    send(6, t, zbo.at[t, 0], zb.at[t, 0], 1, 0),
                    send(7, t, zbo.at[t, 1], zb.at[t, 1], -1, 0),
                ]
            if k == 1:
                sx[t, 2:rows + 2] = section[1]
                copies += [
                    send(4, t, sx.at[t, rows:rows + 2], sx.at[t, 0:2], 0, 1),
                    send(5, t, sx.at[t, 2:4], sx.at[t, rows + 2:rows + 4], 0, -1),
                ]
        joined = stream_first(section[0])
        arrive(copies)
        kept += copies
        met = jnp.concatenate([flat, wide(zb[t, 0]), wide(zb[t, 1])], axis=0)
        source = joined + cross_slope(sx[t]) + tall(dot(form_a[:cells], parts(met)), rows)
        cx[t, low:high] = source
        copies = [
            send(8, t, cx.at[t, low:high], cx.at[t, low - rows:low], 0, 1),
            send(9, t, cx.at[t, low:high], cx.at[t, high:high + rows], 0, -1),
            send(10, t, cx.at[t, high - 1:high], cx.at[t, 0:1], 0, 2),
            send(11, t, cx.at[t, low:low + 1], cx.at[t, high + rows:high + rows + 1], 0, -2),
        ]
        edge = dot(sums_c[...], parts(wide(source)))
        number = 12
        for side in range(2):
            zco[t, side] = tall(edge[side * rc:(side + 1) * rc], rows)
            da = 1 - 2 * side
            copies += [
                send(number, t, zco.at[t, side], zc.at[t, side, low:high], da, 0),
                send(number + 1, t, zco.at[t, side], zc.at[t, side, low - rows:low], da, 1),
                send(number + 2, t, zco.at[t, side], zc.at[t, side, high:high + rows], da, -1),
                send(number + 3, t, zco.at[t, side, rows - 1:rows], zc.at[t, side, 0:1], da, 2),
                send(number + 4, t, zco.at[t, side, 0:1], zc.at[t, side, high + rows:high + rows + 1], da, -2),
            ]
            number += 5
        arrive(copies)
        kept += copies
        joint = jnp.concatenate([cx[t], zc[t, 0], zc[t, 1]], axis=1)
        columns = joint.shape[-1]
        joint = parts(wide(joint))
        powers = dot(form_c[:4 * cells], joint)
        slopes = dot(form_c[4 * cells:], joint[:, 2 * columns:(total - 2) * columns])
        t0, t1, t2, t3 = [tall(powers[i * cells:(i + 1) * cells], total) for i in range(4)]
        d0, d1, d2, d3 = [tall(slopes[i * cells:(i + 1) * cells], total - 4) for i in range(4)]
        x = inside(t2[1:total - 1] + beside(t3), 1 - FAR)
        x = inside(t1[2:total - 2] + beside(x), 2 - FAR)
        scalar = inside(t0[3:total - 3] + beside(x), 3 - FAR)
        n = total - 4
        x = inside(d2[1:n - 1] + beside(d3), 3 - FAR)
        x = inside(d1[2:n - 2] + beside(x), 4 - FAR)
        slope = d0[3:n - 3] + beside(x)
        results = [
            section[0] + stream_first(scalar[2:rows + 2]),
            section[1] + cross_slope(scalar),
            section[2] + slope,
        ]
        for k in range(3):
            if t:
                for y in range(rows):
                    out[k, pl.ds(y, cells, stride=rows), :] = results[k][y]
            else:
                vx[1, k, 2:rows + 2] = results[k]
    for copy, dc in kept:
        there(dc, copy.wait_send)


def solution(mesh):
    spans, crosses = mesh.shape["span"], mesh.shape["cross"]

    def per_device(velocity, viscosity):
        _, cells, rows, columns = velocity.shape
        k1, k2 = symbols(cells * spans)
        g = 1.0 / (4.0 + k2)
        sums_a, form_a = block_form([1j * k1, -k2 + 0j], cells, 8)
        powers = [g ** (m + 1) + 0j for m in range(4)]
        sums_c, form_c = block_form(powers + [1j * k1 * p for p in powers], cells, RANK)
        table = np.concatenate([
            np.pad(part, ((0, 0), (0, form_c.shape[1] - part.shape[1])))
            for part in (sums_a, sums_c, form_a, form_c)
        ])
        table = np.pad(table, ((0, 0), (0, -table.shape[1] % 128)))
        total = rows + 2 * FAR
        f32 = jnp.float32
        hbm = pl.BlockSpec(memory_space=pltpu.HBM)
        vmem = pl.BlockSpec(memory_space=pltpu.VMEM)
        result = pl.pallas_call(
            lambda *refs: kernel(spans, crosses, *refs),
            out_shape=jax.ShapeDtypeStruct((3, cells * rows, columns), f32),
            in_specs=[hbm] * 3,
            out_specs=vmem,
            scratch_shapes=[
                pltpu.VMEM((3, cells * rows, columns), f32),
                pltpu.VMEM((cells * rows, columns), f32),
                pltpu.VMEM(table.shape, f32),
                pltpu.SemaphoreType.DMA((3,)),
                pltpu.VMEM((2, 3, rows + 4, cells, columns), f32),
                pltpu.VMEM((2, 2, 3 * rows, 8, columns), f32),
                pltpu.VMEM((2, 2, 3 * rows, 8, columns), f32),
                pltpu.VMEM((2, rows + 4, cells, columns), f32),
                pltpu.VMEM((2, 2, rows, 8, columns), f32),
                pltpu.VMEM((2, 2, rows, 8, columns), f32),
                pltpu.VMEM((2, total, cells, columns), f32),
                pltpu.VMEM((2, 2, total, RANK, columns), f32),
                pltpu.VMEM((2, 2, rows, RANK, columns), f32),
                pltpu.VMEM((rows, cells, columns), f32),
                pltpu.SemaphoreType.DMA((2, 22)),
                pltpu.SemaphoreType.DMA((2, 22)),
            ],
            compiler_params=pltpu.CompilerParams(
                collective_id=0, has_side_effects=True, vmem_limit_bytes=63 * 1024 * 1024
            ),
        )(
            velocity.reshape(3, cells * rows, columns), viscosity.reshape(cells * rows, columns),
            jnp.asarray(table),
        )
        return result.reshape(3, cells, rows, columns)

    return jax.shard_map(
        per_device,
        mesh=mesh,
        in_specs=(P(None, "span", "cross", None), P("span", "cross", None)),
        out_specs=P(None, "span", "cross", None),
        check_vma=False,
    )
```

```python
import jax
import jax.numpy as jnp
import numpy as np
from jax import lax
from jax.experimental import pallas as pl
from jax.experimental.pallas import tpu as pltpu
from jax.sharding import PartitionSpec as P

MESH = pl.DeviceIdType.MESH
TIME_STEP = 0.1
FAR = 5
RANK = 8


def symbols(length):
    w = 2.0 * np.pi * np.arange(length) / length
    k1 = (14 / 9 * np.sin(w) + 1 / 18 * np.sin(2 * w)) / (1 + 2 / 3 * np.cos(w))
    k2 = (24 / 11 * (1 - np.cos(w)) + 3 / 22 * (1 - np.cos(2 * w))) / (1 + 4 / 11 * np.cos(w))
    return k1, k2


def triple(table):
    high = table.astype(jnp.bfloat16)
    low = (table - high.astype(np.float64)).astype(jnp.bfloat16)
    return np.concatenate([high, low, high], axis=1).astype(np.float32)


def parts(values):
    high = values.astype(jnp.bfloat16)
    low = (values - high.astype(jnp.float32)).astype(jnp.bfloat16)
    return jnp.concatenate([high, high, low], axis=0)


def block_form(table, cells, rank):
    length = table[0].shape[0]
    kernels = [np.fft.ifft(symbol).real for symbol in table]
    offset = np.arange(cells)[:, None] - np.arange(cells)[None, :]
    own = np.concatenate([h[offset % length] for h in kernels])
    left = np.concatenate([h[(offset + cells) % length] for h in kernels])
    right = np.concatenate([h[(offset - cells) % length] for h in kernels])
    to_right = np.linalg.svd(left)[2][:rank]
    to_left = np.linalg.svd(right)[2][:rank]
    sums = np.concatenate([to_right, to_left])
    apply = np.concatenate([own, left @ to_right.T, right @ to_left.T], axis=1)
    return triple(sums), triple(apply)


def turn(values, shift):
    axis = values.ndim - 1
    return pltpu.roll(values, shift % values.shape[axis], axis)


def wide(values):
    return jnp.concatenate([values[i] for i in range(values.shape[0])], axis=-1)


def tall(values, count):
    n = values.shape[-1] // count
    return jnp.stack([values[:, i * n:(i + 1) * n] for i in range(count)])


def stream_pair(values):
    up_one, down_one = turn(values, -1), turn(values, 1)
    up_two, down_two = turn(values, -2), turn(values, 2)
    first = (8.0 * (up_one - down_one) - (up_two - down_two)) * (1.0 / 12.0)
    curve = (16.0 * (up_one + down_one) - (up_two + down_two) - 30.0 * values) * (1.0 / 12.0)
    return first, curve


def stream_first(values):
    return (8.0 * (turn(values, -1) - turn(values, 1)) - (turn(values, -2) - turn(values, 2))) * (1.0 / 12.0)


def cross_slope(p):
    n = p.shape[0]
    return (8.0 * (p[3:n - 1] - p[1:n - 3]) - (p[4:] - p[:n - 4])) * (1.0 / 12.0)


def cross_curve(p):
    n = p.shape[0]
    return (16.0 * (p[3:n - 1] + p[1:n - 3]) - (p[4:] + p[:n - 4]) - 30.0 * p[2:n - 2]) * (1.0 / 12.0)


def beside(p):
    mid = p[1:p.shape[0] - 1]
    return turn(mid, 1) + turn(mid, -1) + p[2:] + p[:p.shape[0] - 2]


def kernel(spans, crosses, vel_hbm, visc_hbm, table_hbm, out, vel, visc, table, load_sem,
           vx, za, zao, sx, zb, zbo, cx, zc, zco, nu_ref, send_sem, recv_sem):
    a, c = lax.axis_index("span"), lax.axis_index("cross")
    rows, cells = nu_ref.shape[0], nu_ref.shape[1]
    ra = rc = RANK
    loads = [
        pltpu.make_async_copy(source, target, load_sem.at[i])
        for i, (source, target) in enumerate([(vel_hbm, vel), (visc_hbm, visc), (table_hbm, table)])
    ]
    for load in loads:
        load.start()
    n_sums = 2 * RANK
    sums_a = table.at[0:n_sums]
    sums_c = table.at[n_sums:2 * n_sums]
    form_a = table.at[2 * n_sums:2 * n_sums + 2 * cells]
    form_c = table.at[2 * n_sums + 2 * cells:]

    def device(da, dc):
        return lax.rem(a + (da + spans), spans), lax.rem(c + (dc + crosses), crosses)

    def there(dc, action):
        if dc == 0:
            action()
        else:
            pl.when((c + dc >= 0) & (c + dc < crosses))(action)

    def clear(dc, refs):
        def action():
            for ref in refs:
                ref[...] = jnp.zeros(ref.shape, ref.dtype)

        pl.when((c + dc < 0) | (c + dc >= crosses))(action)

    barrier = pltpu.get_barrier_semaphore()
    greeted = [(da, dc) for da in (-1, 0, 1) for dc in (-2, -1, 0, 1, 2) if (da, dc) != (0, 0)]
    for da, dc in greeted:
        pl.semaphore_signal(barrier, inc=1, device_id=device(da, dc), device_id_type=MESH)

    def send(number, section, src, dst, da, dc):
        copy = pltpu.make_async_remote_copy(
            src_ref=src, dst_ref=dst, send_sem=send_sem.at[section, number],
            recv_sem=recv_sem.at[section, number], device_id=device(da, dc), device_id_type=MESH,
        )
        there(dc, copy.start)
        return copy, dc

    def arrive(copies):
        for copy, dc in copies:
            there(-dc, copy.wait_recv)

    def inside(values, first):
        kept_rows = []
        for i in range(values.shape[0]):
            number = first + i
            if number < 0:
                kept_rows.append(jnp.where(c * rows + number >= 0, values[i], 0.0))
            elif number >= rows:
                kept_rows.append(jnp.where(c * rows + number < rows * crosses, values[i], 0.0))
            else:
                kept_rows.append(values[i])
        return jnp.stack(kept_rows)

    def dot(left, right):
        rest = jnp.zeros((left.shape[1] - right.shape[0], right.shape[1]), right.dtype)
        right = jnp.concatenate([right, rest], axis=0)
        return jnp.dot(left.astype(jnp.bfloat16), right, preferred_element_type=jnp.float32)

    low, high = FAR, FAR + rows
    total = rows + 2 * FAR
    clear(-1, [vx.at[:, :, 0:2], sx.at[:, 0:2], cx.at[:, low - rows:low], zc.at[:, :, low - rows:low]])
    clear(1, [vx.at[:, :, rows + 2:], sx.at[:, rows + 2:], cx.at[:, high:high + rows], zc.at[:, :, high:high + rows]])
    clear(-2, [cx.at[:, 0:1], zc.at[:, :, 0:1]])
    clear(2, [cx.at[:, total - 1:], zc.at[:, :, total - 1:]])
    for load in loads:
        load.wait()
    for y in range(rows):
        own = pl.ds(y, cells, stride=rows)
        for k in range(3):
            vx[0, k, y + 2] = vel[k, own, :]
        nu_ref[y] = visc[own, :]

    def start(t, first, last, number):
        ends = slice(first * rows, last * rows)
        sent = [
            send(number, t, vx.at[t, first:last, rows:rows + 2], vx.at[t, first:last, 0:2], 0, 1),
            send(number + 1, t, vx.at[t, first:last, 2:4], vx.at[t, first:last, rows + 2:rows + 4], 0, -1),
        ]
        values = vx[t, first:last, 2:rows + 2]
        values = values.reshape((last - first) * rows, cells, values.shape[-1])
        edge = dot(sums_a[...], parts(wide(values)))
        zao[t, 0, ends] = tall(edge[:ra], values.shape[0])
        zao[t, 1, ends] = tall(edge[ra:], values.shape[0])
        sent += [
            send(number + 2, t, zao.at[t, 0, ends], za.at[t, 0, ends], 1, 0),
            send(number + 3, t, zao.at[t, 1, ends], za.at[t, 1, ends], -1, 0),
        ]
        return sent

    kept = []
    for t in range(2):
        if not t:
            pl.semaphore_wait(barrier, len(greeted))
            started = start(0, 0, 3, 0)
        copies = started
        base = vx[t, :, 2:rows + 2]
        flat = wide(base.reshape(3 * rows, cells, base.shape[-1]))
        slope_x, curve_x = stream_pair(base.reshape(3 * rows, cells, base.shape[-1]))
        arrive(copies)
        kept += copies
        met = jnp.concatenate([flat, wide(za[t, 0]), wide(za[t, 1])], axis=0)
        pair = dot(form_a[...], parts(met))
        slope_z = tall(pair[:cells], 3 * rows)
        curve_z = tall(pair[cells:], 3 * rows)
        section = [None] * 3
        nu = nu_ref[...]
        copies = []
        for k in (2, 1, 0):
            padded = vx[t, k]
            at = slice(k * rows, (k + 1) * rows)
            rate = nu * (curve_x[at] + cross_curve(padded) + curve_z[at]) - (
                base[0] * slope_x[at] + base[1] * cross_slope(padded) + base[2] * slope_z[at])
            if t:
                section[k] = 0.5 * vx[0, k, 2:rows + 2] + 0.5 * (base[k] + TIME_STEP * rate)
            else:
                section[k] = base[k] + TIME_STEP * rate
            if k == 2:
                flat = wide(section[2])
                edge = dot(sums_a[...], parts(flat))
                zbo[t, 0] = tall(edge[:ra], rows)
                zbo[t, 1] = tall(edge[ra:], rows)
                copies += [
                    send(6, t, zbo.at[t, 0], zb.at[t, 0], 1, 0),
                    send(7, t, zbo.at[t, 1], zb.at[t, 1], -1, 0),
                ]
            if k == 1:
                sx[t, 2:rows + 2] = section[1]
                copies += [
                    send(4, t, sx.at[t, rows:rows + 2], sx.at[t, 0:2], 0, 1),
                    send(5, t, sx.at[t, 2:4], sx.at[t, rows + 2:rows + 4], 0, -1),
                ]
        joined = stream_first(section[0])
        arrive(copies)
        kept += copies
        met = jnp.concatenate([flat, wide(zb[t, 0]), wide(zb[t, 1])], axis=0)
        source = joined + cross_slope(sx[t]) + tall(dot(form_a[:cells], parts(met)), rows)
        cx[t, low:high] = source
        copies = [
            send(8, t, cx.at[t, low:high], cx.at[t, low - rows:low], 0, 1),
            send(9, t, cx.at[t, low:high], cx.at[t, high:high + rows], 0, -1),
            send(10, t, cx.at[t, high - 1:high], cx.at[t, 0:1], 0, 2),
            send(11, t, cx.at[t, low:low + 1], cx.at[t, high + rows:high + rows + 1], 0, -2),
        ]
        edge = dot(sums_c[...], parts(wide(source)))
        number = 12
        for side in range(2):
            zco[t, side] = tall(edge[side * rc:(side + 1) * rc], rows)
            da = 1 - 2 * side
            copies += [
                send(number, t, zco.at[t, side], zc.at[t, side, low:high], da, 0),
                send(number + 1, t, zco.at[t, side], zc.at[t, side, low - rows:low], da, 1),
                send(number + 2, t, zco.at[t, side], zc.at[t, side, high:high + rows], da, -1),
                send(number + 3, t, zco.at[t, side, rows - 1:rows], zc.at[t, side, 0:1], da, 2),
                send(number + 4, t, zco.at[t, side, 0:1], zc.at[t, side, high + rows:high + rows + 1], da, -2),
            ]
            number += 5
        arrive(copies)
        kept += copies
        joint = jnp.concatenate([cx[t], zc[t, 0], zc[t, 1]], axis=1)
        columns = joint.shape[-1]
        joint = parts(wide(joint))
        powers = dot(form_c[:4 * cells], joint)
        t0, t1, t2, t3 = [tall(powers[i * cells:(i + 1) * cells], total) for i in range(4)]
        x = inside(t2[1:total - 1] + beside(t3), 1 - FAR)
        x = inside(t1[2:total - 2] + beside(x), 2 - FAR)
        scalar = inside(t0[3:total - 3] + beside(x), 3 - FAR)
        results = [section[0] + stream_first(scalar[2:rows + 2]), section[1] + cross_slope(scalar)]
        for k in range(2):
            if t:
                out[k] = results[k]
            else:
                vx[1, k, 2:rows + 2] = results[k]
        if not t:
            started = start(1, 0, 2, 0)
        slopes = dot(form_c[4 * cells:], joint[:, 2 * columns:(total - 2) * columns])
        d0, d1, d2, d3 = [tall(slopes[i * cells:(i + 1) * cells], total - 4) for i in range(4)]
        n = total - 4
        x = inside(d2[1:n - 1] + beside(d3), 3 - FAR)
        x = inside(d1[2:n - 2] + beside(x), 4 - FAR)
        slope = d0[3:n - 3] + beside(x)
        if t:
            out[2] = section[2] + slope
        else:
            vx[1, 2, 2:rows + 2] = section[2] + slope
            started = started + start(1, 2, 3, 22)
    for copy, dc in kept:
        there(dc, copy.wait_send)


def solution(mesh):
    spans, crosses = mesh.shape["span"], mesh.shape["cross"]

    def per_device(velocity, viscosity):
        _, cells, rows, columns = velocity.shape
        k1, k2 = symbols(cells * spans)
        g = 1.0 / (4.0 + k2)
        sums_a, form_a = block_form([1j * k1, -k2 + 0j], cells, 8)
        powers = [g ** (m + 1) + 0j for m in range(4)]
        sums_c, form_c = block_form(powers + [1j * k1 * p for p in powers], cells, RANK)
        table = np.concatenate([
            np.pad(part, ((0, 0), (0, form_c.shape[1] - part.shape[1])))
            for part in (sums_a, sums_c, form_a, form_c)
        ])
        table = np.pad(table, ((0, 0), (0, -table.shape[1] % 128)))
        total = rows + 2 * FAR
        f32 = jnp.float32
        hbm = pl.BlockSpec(memory_space=pltpu.HBM)
        vmem = pl.BlockSpec(memory_space=pltpu.VMEM)
        result = pl.pallas_call(
            lambda *refs: kernel(spans, crosses, *refs),
            out_shape=jax.ShapeDtypeStruct((3, rows, cells, columns), f32),
            in_specs=[hbm] * 3,
            out_specs=vmem,
            scratch_shapes=[
                pltpu.VMEM((3, cells * rows, columns), f32),
                pltpu.VMEM((cells * rows, columns), f32),
                pltpu.VMEM(table.shape, f32),
                pltpu.SemaphoreType.DMA((3,)),
                pltpu.VMEM((2, 3, rows + 4, cells, columns), f32),
                pltpu.VMEM((2, 2, 3 * rows, 8, columns), f32),
                pltpu.VMEM((2, 2, 3 * rows, 8, columns), f32),
                pltpu.VMEM((2, rows + 4, cells, columns), f32),
                pltpu.VMEM((2, 2, rows, 8, columns), f32),
                pltpu.VMEM((2, 2, rows, 8, columns), f32),
                pltpu.VMEM((2, total, cells, columns), f32),
                pltpu.VMEM((2, 2, total, RANK, columns), f32),
                pltpu.VMEM((2, 2, rows, RANK, columns), f32),
                pltpu.VMEM((rows, cells, columns), f32),
                pltpu.SemaphoreType.DMA((2, 26)),
                pltpu.SemaphoreType.DMA((2, 26)),
            ],
            compiler_params=pltpu.CompilerParams(
                collective_id=0, has_side_effects=True, vmem_limit_bytes=63 * 1024 * 1024
            ),
        )(
            velocity.reshape(3, cells * rows, columns), viscosity.reshape(cells * rows, columns),
            jnp.asarray(table),
        )
        return result.transpose(0, 2, 1, 3)

    return jax.shard_map(
        per_device,
        mesh=mesh,
        in_specs=(P(None, "span", "cross", None), P("span", "cross", None)),
        out_specs=P(None, "span", "cross", None),
        check_vma=False,
    )
```

```python
import jax
import jax.numpy as jnp
import numpy as np
from jax import lax
from jax.experimental import pallas as pl
from jax.experimental.pallas import tpu as pltpu
from jax.sharding import PartitionSpec as P

MESH = pl.DeviceIdType.MESH
TIME_STEP = 0.1
FAR = 5
RANK = 8


def symbols(length):
    w = 2.0 * np.pi * np.arange(length) / length
    k1 = (14 / 9 * np.sin(w) + 1 / 18 * np.sin(2 * w)) / (1 + 2 / 3 * np.cos(w))
    k2 = (24 / 11 * (1 - np.cos(w)) + 3 / 22 * (1 - np.cos(2 * w))) / (1 + 4 / 11 * np.cos(w))
    return k1, k2


def triple(table):
    high = table.astype(jnp.bfloat16)
    low = (table - high.astype(np.float64)).astype(jnp.bfloat16)
    return np.concatenate([high, low, high], axis=1).astype(np.float32)


def parts(values):
    high = values.astype(jnp.bfloat16)
    low = (values - high.astype(jnp.float32)).astype(jnp.bfloat16)
    return jnp.concatenate([high, high, low], axis=0)


def block_form(table, cells, rank):
    length = table[0].shape[0]
    kernels = [np.fft.ifft(symbol).real for symbol in table]
    offset = np.arange(cells)[:, None] - np.arange(cells)[None, :]
    own = np.concatenate([h[offset % length] for h in kernels])
    left = np.concatenate([h[(offset + cells) % length] for h in kernels])
    right = np.concatenate([h[(offset - cells) % length] for h in kernels])
    to_right = np.linalg.svd(left)[2][:rank]
    to_left = np.linalg.svd(right)[2][:rank]
    sums = np.concatenate([to_right, to_left])
    apply = np.concatenate([own, left @ to_right.T, right @ to_left.T], axis=1)
    return triple(sums), triple(apply)


def turn(values, shift):
    axis = values.ndim - 1
    return pltpu.roll(values, shift % values.shape[axis], axis)


def wide(values):
    return jnp.concatenate([values[i] for i in range(values.shape[0])], axis=-1)


def tall(values, count):
    n = values.shape[-1] // count
    return jnp.stack([values[:, i * n:(i + 1) * n] for i in range(count)])


def stream_pair(values):
    up_one, down_one = turn(values, -1), turn(values, 1)
    up_two, down_two = turn(values, -2), turn(values, 2)
    first = (8.0 * (up_one - down_one) - (up_two - down_two)) * (1.0 / 12.0)
    curve = (16.0 * (up_one + down_one) - (up_two + down_two) - 30.0 * values) * (1.0 / 12.0)
    return first, curve


def stream_first(values):
    return (8.0 * (turn(values, -1) - turn(values, 1)) - (turn(values, -2) - turn(values, 2))) * (1.0 / 12.0)


def cross_slope(p):
    n = p.shape[0]
    return (8.0 * (p[3:n - 1] - p[1:n - 3]) - (p[4:] - p[:n - 4])) * (1.0 / 12.0)


def cross_curve(p):
    n = p.shape[0]
    return (16.0 * (p[3:n - 1] + p[1:n - 3]) - (p[4:] + p[:n - 4]) - 30.0 * p[2:n - 2]) * (1.0 / 12.0)


def beside(p):
    mid = p[1:p.shape[0] - 1]
    return turn(mid, 1) + turn(mid, -1) + p[2:] + p[:p.shape[0] - 2]


def kernel(spans, crosses, vel_hbm, visc_hbm, table_hbm, out, vel, visc, table, load_sem,
           vx, za, zao, sx, zb, zbo, cx, zc, zco, nu_ref, send_sem, recv_sem):
    a, c = lax.axis_index("span"), lax.axis_index("cross")
    rows, cells = nu_ref.shape[0], nu_ref.shape[1]
    ra = rc = RANK
    loads = [
        pltpu.make_async_copy(source, target, load_sem.at[i])
        for i, (source, target) in enumerate([(vel_hbm, vel), (visc_hbm, visc), (table_hbm, table)])
    ]
    for load in loads:
        load.start()
    n_sums = 2 * RANK
    sums_a = table.at[0:n_sums]
    sums_c = table.at[n_sums:2 * n_sums]
    form_a = table.at[2 * n_sums:2 * n_sums + 2 * cells]
    form_c = table.at[2 * n_sums + 2 * cells:]

    def device(da, dc):
        return lax.rem(a + (da + spans), spans), lax.rem(c + (dc + crosses), crosses)

    def there(dc, action):
        if dc == 0:
            action()
        else:
            pl.when((c + dc >= 0) & (c + dc < crosses))(action)

    def clear(dc, refs):
        def action():
            for ref in refs:
                ref[...] = jnp.zeros(ref.shape, ref.dtype)

        pl.when((c + dc < 0) | (c + dc >= crosses))(action)

    barrier = pltpu.get_barrier_semaphore()
    greeted = [(da, dc) for da in (-1, 0, 1) for dc in (-2, -1, 0, 1, 2) if (da, dc) != (0, 0)]
    for da, dc in greeted:
        pl.semaphore_signal(barrier, inc=1, device_id=device(da, dc), device_id_type=MESH)

    def send(number, section, src, dst, da, dc):
        copy = pltpu.make_async_remote_copy(
            src_ref=src, dst_ref=dst, send_sem=send_sem.at[section, number],
            recv_sem=recv_sem.at[section, number], device_id=device(da, dc), device_id_type=MESH,
        )
        there(dc, copy.start)
        return copy, dc

    def arrive(copies):
        for copy, dc in copies:
            there(-dc, copy.wait_recv)

    def inside(values, first):
        kept_rows = []
        for i in range(values.shape[0]):
            number = first + i
            if number < 0:
                kept_rows.append(jnp.where(c * rows + number >= 0, values[i], 0.0))
            elif number >= rows:
                kept_rows.append(jnp.where(c * rows + number < rows * crosses, values[i], 0.0))
            else:
                kept_rows.append(values[i])
        return jnp.stack(kept_rows)

    def dot(left, right):
        rest = jnp.zeros((left.shape[1] - right.shape[0], right.shape[1]), right.dtype)
        right = jnp.concatenate([right, rest], axis=0)
        return jnp.dot(left.astype(jnp.bfloat16), right, preferred_element_type=jnp.float32)

    low, high = FAR, FAR + rows
    total = rows + 2 * FAR
    clear(-1, [vx.at[:, :, 0:2], sx.at[:, 0:2], cx.at[:, low - rows:low], zc.at[:, :, low - rows:low]])
    clear(1, [vx.at[:, :, rows + 2:], sx.at[:, rows + 2:], cx.at[:, high:high + rows], zc.at[:, :, high:high + rows]])
    clear(-2, [cx.at[:, 0:1], zc.at[:, :, 0:1]])
    clear(2, [cx.at[:, total - 1:], zc.at[:, :, total - 1:]])
    for load in loads:
        load.wait()
    for y in range(rows):
        own = pl.ds(y, cells, stride=rows)
        for k in range(3):
            vx[0, k, y + 2] = vel[k, own, :]
        nu_ref[y] = visc[own, :]

    def start(t, first, last, number):
        ends = slice(first * rows, last * rows)
        sent = [
            send(number, t, vx.at[t, first:last, rows:rows + 2], vx.at[t, first:last, 0:2], 0, 1),
            send(number + 1, t, vx.at[t, first:last, 2:4], vx.at[t, first:last, rows + 2:rows + 4], 0, -1),
        ]
        values = vx[t, first:last, 2:rows + 2]
        values = values.reshape((last - first) * rows, cells, values.shape[-1])
        edge = dot(sums_a[...], parts(wide(values)))
        zao[t, 0, ends] = tall(edge[:ra], values.shape[0])
        zao[t, 1, ends] = tall(edge[ra:], values.shape[0])
        sent += [
            send(number + 2, t, zao.at[t, 0, ends], za.at[t, 0, ends], 1, 0),
            send(number + 3, t, zao.at[t, 1, ends], za.at[t, 1, ends], -1, 0),
        ]
        return sent

    def deliver(k, result):
        for y in range(rows):
            out[k, pl.ds(y, cells, stride=rows), :] = result[y]

    kept = []
    for t in range(2):
        if not t:
            pl.semaphore_wait(barrier, len(greeted))
            started = start(0, 0, 3, 0)
        copies = started
        base = vx[t, :, 2:rows + 2]
        flat = wide(base.reshape(3 * rows, cells, base.shape[-1]))
        slope_x, curve_x = stream_pair(base.reshape(3 * rows, cells, base.shape[-1]))
        nu = nu_ref[...]
        early = [
            nu * curve_x[k * rows:(k + 1) * rows] - base[0] * slope_x[k * rows:(k + 1) * rows]
            for k in range(3)
        ]
        arrive(copies)
        kept += copies
        met = jnp.concatenate([flat, wide(za[t, 0]), wide(za[t, 1])], axis=0)
        pair = dot(form_a[...], parts(met))
        slope_z = tall(pair[:cells], 3 * rows)
        curve_z = tall(pair[cells:], 3 * rows)
        section = [None] * 3
        copies = []
        for k in (2, 1, 0):
            padded = vx[t, k]
            at = slice(k * rows, (k + 1) * rows)
            rate = early[k] + nu * (cross_curve(padded) + curve_z[at]) - (
                base[1] * cross_slope(padded) + base[2] * slope_z[at])
            if t:
                section[k] = 0.5 * vx[0, k, 2:rows + 2] + 0.5 * (base[k] + TIME_STEP * rate)
            else:
                section[k] = base[k] + TIME_STEP * rate
            if k == 2:
                flat = wide(section[2])
                edge = dot(sums_a[...], parts(flat))
                zbo[t, 0] = tall(edge[:ra], rows)
                zbo[t, 1] = tall(edge[ra:], rows)
                copies += [
                    send(6, t, zbo.at[t, 0], zb.at[t, 0], 1, 0),
                    send(7, t, zbo.at[t, 1], zb.at[t, 1], -1, 0),
                ]
            if k == 1:
                sx[t, 2:rows + 2] = section[1]
                copies += [
                    send(4, t, sx.at[t, rows:rows + 2], sx.at[t, 0:2], 0, 1),
                    send(5, t, sx.at[t, 2:4], sx.at[t, rows + 2:rows + 4], 0, -1),
                ]
        joined = stream_first(section[0])
        arrive(copies)
        kept += copies
        met = jnp.concatenate([flat, wide(zb[t, 0]), wide(zb[t, 1])], axis=0)
        source = joined + cross_slope(sx[t]) + tall(dot(form_a[:cells], parts(met)), rows)
        cx[t, low:high] = source
        copies = [
            send(8, t, cx.at[t, low:high], cx.at[t, low - rows:low], 0, 1),
            send(9, t, cx.at[t, low:high], cx.at[t, high:high + rows], 0, -1),
            send(10, t, cx.at[t, high - 1:high], cx.at[t, 0:1], 0, 2),
            send(11, t, cx.at[t, low:low + 1], cx.at[t, high + rows:high + rows + 1], 0, -2),
        ]
        edge = dot(sums_c[...], parts(wide(source)))
        number = 12
        for side in range(2):
            zco[t, side] = tall(edge[side * rc:(side + 1) * rc], rows)
            da = 1 - 2 * side
            copies += [
                send(number, t, zco.at[t, side], zc.at[t, side, low:high], da, 0),
                send(number + 1, t, zco.at[t, side], zc.at[t, side, low - rows:low], da, 1),
                send(number + 2, t, zco.at[t, side], zc.at[t, side, high:high + rows], da, -1),
                send(number + 3, t, zco.at[t, side, rows - 1:rows], zc.at[t, side, 0:1], da, 2),
                send(number + 4, t, zco.at[t, side, 0:1], zc.at[t, side, high + rows:high + rows + 1], da, -2),
            ]
            number += 5
        arrive(copies)
        kept += copies
        joint = jnp.concatenate([cx[t], zc[t, 0], zc[t, 1]], axis=1)
        columns = joint.shape[-1]
        joint = parts(wide(joint))
        powers = dot(form_c[:4 * cells], joint)
        t0, t1, t2, t3 = [tall(powers[i * cells:(i + 1) * cells], total) for i in range(4)]
        x = inside(t2[1:total - 1] + beside(t3), 1 - FAR)
        x = inside(t1[2:total - 2] + beside(x), 2 - FAR)
        scalar = inside(t0[3:total - 3] + beside(x), 3 - FAR)
        results = [section[0] + stream_first(scalar[2:rows + 2]), section[1] + cross_slope(scalar)]
        for k in range(2):
            if t:
                deliver(k, results[k])
            else:
                vx[1, k, 2:rows + 2] = results[k]
        if not t:
            started = start(1, 0, 2, 0)
        slopes = dot(form_c[4 * cells:], joint[:, 2 * columns:(total - 2) * columns])
        d0, d1, d2, d3 = [tall(slopes[i * cells:(i + 1) * cells], total - 4) for i in range(4)]
        n = total - 4
        x = inside(d2[1:n - 1] + beside(d3), 3 - FAR)
        x = inside(d1[2:n - 2] + beside(x), 4 - FAR)
        slope = d0[3:n - 3] + beside(x)
        if t:
            deliver(2, section[2] + slope)
        else:
            vx[1, 2, 2:rows + 2] = section[2] + slope
            started = started + start(1, 2, 3, 22)
    for copy, dc in kept:
        there(dc, copy.wait_send)


def solution(mesh):
    spans, crosses = mesh.shape["span"], mesh.shape["cross"]

    def per_device(velocity, viscosity):
        _, cells, rows, columns = velocity.shape
        k1, k2 = symbols(cells * spans)
        g = 1.0 / (4.0 + k2)
        sums_a, form_a = block_form([1j * k1, -k2 + 0j], cells, 8)
        powers = [g ** (m + 1) + 0j for m in range(4)]
        sums_c, form_c = block_form(powers + [1j * k1 * p for p in powers], cells, RANK)
        table = np.concatenate([
            np.pad(part, ((0, 0), (0, form_c.shape[1] - part.shape[1])))
            for part in (sums_a, sums_c, form_a, form_c)
        ])
        table = np.pad(table, ((0, 0), (0, -table.shape[1] % 128)))
        total = rows + 2 * FAR
        f32 = jnp.float32
        hbm = pl.BlockSpec(memory_space=pltpu.HBM)
        vmem = pl.BlockSpec(memory_space=pltpu.VMEM)
        result = pl.pallas_call(
            lambda *refs: kernel(spans, crosses, *refs),
            out_shape=jax.ShapeDtypeStruct((3, cells * rows, columns), f32),
            in_specs=[hbm] * 3,
            out_specs=vmem,
            scratch_shapes=[
                pltpu.VMEM((3, cells * rows, columns), f32),
                pltpu.VMEM((cells * rows, columns), f32),
                pltpu.VMEM(table.shape, f32),
                pltpu.SemaphoreType.DMA((3,)),
                pltpu.VMEM((2, 3, rows + 4, cells, columns), f32),
                pltpu.VMEM((2, 2, 3 * rows, 8, columns), f32),
                pltpu.VMEM((2, 2, 3 * rows, 8, columns), f32),
                pltpu.VMEM((2, rows + 4, cells, columns), f32),
                pltpu.VMEM((2, 2, rows, 8, columns), f32),
                pltpu.VMEM((2, 2, rows, 8, columns), f32),
                pltpu.VMEM((2, total, cells, columns), f32),
                pltpu.VMEM((2, 2, total, RANK, columns), f32),
                pltpu.VMEM((2, 2, rows, RANK, columns), f32),
                pltpu.VMEM((rows, cells, columns), f32),
                pltpu.SemaphoreType.DMA((2, 26)),
                pltpu.SemaphoreType.DMA((2, 26)),
            ],
            compiler_params=pltpu.CompilerParams(
                collective_id=0, has_side_effects=True, vmem_limit_bytes=63 * 1024 * 1024
            ),
        )(
            velocity.reshape(3, cells * rows, columns), viscosity.reshape(cells * rows, columns),
            jnp.asarray(table),
        )
        return result.reshape(3, cells, rows, columns)

    return jax.shard_map(
        per_device,
        mesh=mesh,
        in_specs=(P(None, "span", "cross", None), P("span", "cross", None)),
        out_specs=P(None, "span", "cross", None),
        check_vma=False,
    )
```

```python
import jax
import jax.numpy as jnp
import numpy as np
from jax import lax
from jax.experimental import pallas as pl
from jax.experimental.pallas import tpu as pltpu
from jax.sharding import PartitionSpec as P

MESH = pl.DeviceIdType.MESH
TIME_STEP = 0.1
FAR = 5
RANK = 8


def symbols(length):
    w = 2.0 * np.pi * np.arange(length) / length
    k1 = (14 / 9 * np.sin(w) + 1 / 18 * np.sin(2 * w)) / (1 + 2 / 3 * np.cos(w))
    k2 = (24 / 11 * (1 - np.cos(w)) + 3 / 22 * (1 - np.cos(2 * w))) / (1 + 4 / 11 * np.cos(w))
    return k1, k2


def triple(table):
    high = table.astype(jnp.bfloat16)
    low = (table - high.astype(np.float64)).astype(jnp.bfloat16)
    return np.concatenate([high, low, high], axis=1).astype(np.float32)


def parts(values):
    high = values.astype(jnp.bfloat16)
    low = (values - high.astype(jnp.float32)).astype(jnp.bfloat16)
    return jnp.concatenate([high, high, low], axis=0)


def block_form(table, cells, rank):
    length = table[0].shape[0]
    kernels = [np.fft.ifft(symbol).real for symbol in table]
    offset = np.arange(cells)[:, None] - np.arange(cells)[None, :]
    own = np.concatenate([h[offset % length] for h in kernels])
    left = np.concatenate([h[(offset + cells) % length] for h in kernels])
    right = np.concatenate([h[(offset - cells) % length] for h in kernels])
    to_right = np.linalg.svd(left)[2][:rank]
    to_left = np.linalg.svd(right)[2][:rank]
    sums = np.concatenate([to_right, to_left])
    apply = np.concatenate([own, left @ to_right.T, right @ to_left.T], axis=1)
    return triple(sums), triple(apply)


def turn(values, shift):
    axis = values.ndim - 1
    return pltpu.roll(values, shift % values.shape[axis], axis)


def wide(values):
    return jnp.concatenate([values[i] for i in range(values.shape[0])], axis=-1)


def tall(values, count):
    n = values.shape[-1] // count
    return jnp.stack([values[:, i * n:(i + 1) * n] for i in range(count)])


def stream_pair(values):
    up_one, down_one = turn(values, -1), turn(values, 1)
    up_two, down_two = turn(values, -2), turn(values, 2)
    first = (8.0 * (up_one - down_one) - (up_two - down_two)) * (1.0 / 12.0)
    curve = (16.0 * (up_one + down_one) - (up_two + down_two) - 30.0 * values) * (1.0 / 12.0)
    return first, curve


def stream_first(values):
    return (8.0 * (turn(values, -1) - turn(values, 1)) - (turn(values, -2) - turn(values, 2))) * (1.0 / 12.0)


def cross_slope(p):
    n = p.shape[0]
    return (8.0 * (p[3:n - 1] - p[1:n - 3]) - (p[4:] - p[:n - 4])) * (1.0 / 12.0)


def cross_curve(p):
    n = p.shape[0]
    return (16.0 * (p[3:n - 1] + p[1:n - 3]) - (p[4:] + p[:n - 4]) - 30.0 * p[2:n - 2]) * (1.0 / 12.0)


def beside(p):
    mid = p[1:p.shape[0] - 1]
    return turn(mid, 1) + turn(mid, -1) + p[2:] + p[:p.shape[0] - 2]


def kernel(spans, crosses, vel_hbm, visc_hbm, table_hbm, out, vel, visc, table, load_sem,
           vx, za, zao, sx, zb, zbo, cx, zc, zco, nu_ref, send_sem, recv_sem):
    a, c = lax.axis_index("span"), lax.axis_index("cross")
    rows, cells = nu_ref.shape[0], nu_ref.shape[1]
    ra = rc = RANK
    loads = [
        pltpu.make_async_copy(source, target, load_sem.at[i])
        for i, (source, target) in enumerate([(vel_hbm, vel), (visc_hbm, visc), (table_hbm, table)])
    ]
    for load in loads:
        load.start()
    n_sums = 2 * RANK
    sums_a = table.at[0:n_sums]
    sums_c = table.at[n_sums:2 * n_sums]
    form_a = table.at[2 * n_sums:2 * n_sums + 2 * cells]
    form_c = table.at[2 * n_sums + 2 * cells:]

    def device(da, dc):
        return lax.rem(a + (da + spans), spans), lax.rem(c + (dc + crosses), crosses)

    def there(dc, action):
        if dc == 0:
            action()
        else:
            pl.when((c + dc >= 0) & (c + dc < crosses))(action)

    def clear(dc, refs):
        def action():
            for ref in refs:
                ref[...] = jnp.zeros(ref.shape, ref.dtype)

        pl.when((c + dc < 0) | (c + dc >= crosses))(action)

    barrier = pltpu.get_barrier_semaphore()
    greeted = [(da, dc) for da in (-1, 0, 1) for dc in (-2, -1, 0, 1, 2) if (da, dc) != (0, 0)]
    for da, dc in greeted:
        pl.semaphore_signal(barrier, inc=1, device_id=device(da, dc), device_id_type=MESH)

    def send(number, section, src, dst, da, dc):
        copy = pltpu.make_async_remote_copy(
            src_ref=src, dst_ref=dst, send_sem=send_sem.at[section, number],
            recv_sem=recv_sem.at[section, number], device_id=device(da, dc), device_id_type=MESH,
        )
        there(dc, copy.start)
        return copy, dc

    def arrive(copies):
        for copy, dc in copies:
            there(-dc, copy.wait_recv)

    def inside(values, first):
        kept_rows = []
        for i in range(values.shape[0]):
            number = first + i
            if number < 0:
                kept_rows.append(jnp.where(c * rows + number >= 0, values[i], 0.0))
            elif number >= rows:
                kept_rows.append(jnp.where(c * rows + number < rows * crosses, values[i], 0.0))
            else:
                kept_rows.append(values[i])
        return jnp.stack(kept_rows)

    def dot(left, right):
        rest = jnp.zeros((left.shape[1] - right.shape[0], right.shape[1]), right.dtype)
        right = jnp.concatenate([right, rest], axis=0)
        return jnp.dot(left.astype(jnp.bfloat16), right, preferred_element_type=jnp.float32)

    low, high = FAR, FAR + rows
    total = rows + 2 * FAR
    clear(-1, [vx.at[:, :, 0:2], sx.at[:, 0:2], cx.at[:, low - rows:low], zc.at[:, :, low - rows:low]])
    clear(1, [vx.at[:, :, rows + 2:], sx.at[:, rows + 2:], cx.at[:, high:high + rows], zc.at[:, :, high:high + rows]])
    clear(-2, [cx.at[:, 0:1], zc.at[:, :, 0:1]])
    clear(2, [cx.at[:, total - 1:], zc.at[:, :, total - 1:]])
    for load in loads:
        load.wait()
    for y in range(rows):
        own = pl.ds(y, cells, stride=rows)
        for k in range(3):
            vx[0, k, y + 2] = vel[k, own, :]
        nu_ref[y] = visc[own, :]

    def start(t, first, last, number):
        ends = slice(first * rows, last * rows)
        sent = [
            send(number, t, vx.at[t, first:last, rows:rows + 2], vx.at[t, first:last, 0:2], 0, 1),
            send(number + 1, t, vx.at[t, first:last, 2:4], vx.at[t, first:last, rows + 2:rows + 4], 0, -1),
        ]
        values = vx[t, first:last, 2:rows + 2]
        values = values.reshape((last - first) * rows, cells, values.shape[-1])
        edge = dot(sums_a[...], parts(wide(values)))
        zao[t, 0, ends] = tall(edge[:ra], values.shape[0])
        zao[t, 1, ends] = tall(edge[ra:], values.shape[0])
        sent += [
            send(number + 2, t, zao.at[t, 0, ends], za.at[t, 0, ends], 1, 0),
            send(number + 3, t, zao.at[t, 1, ends], za.at[t, 1, ends], -1, 0),
        ]
        return sent

    def deliver(k, result):
        for y in range(rows):
            out[k, pl.ds(y, cells, stride=rows), :] = result[y]

    kept = []
    for t in range(2):
        if not t:
            pl.semaphore_wait(barrier, len(greeted))
            started = start(0, 0, 3, 0)
        copies = started
        base = vx[t, :, 2:rows + 2]
        flat = wide(base.reshape(3 * rows, cells, base.shape[-1]))
        slope_x, curve_x = stream_pair(base.reshape(3 * rows, cells, base.shape[-1]))
        nu = nu_ref[...]
        early = [
            nu * curve_x[k * rows:(k + 1) * rows] - base[0] * slope_x[k * rows:(k + 1) * rows]
            for k in range(3)
        ]
        arrive(copies)
        kept += copies
        met = jnp.concatenate([flat, wide(za[t, 0]), wide(za[t, 1])], axis=0)
        pair = dot(form_a[...], parts(met))
        slope_z = tall(pair[:cells], 3 * rows)
        curve_z = tall(pair[cells:], 3 * rows)
        section = [None] * 3
        copies = []
        for k in (2, 1, 0):
            padded = vx[t, k]
            at = slice(k * rows, (k + 1) * rows)
            rate = early[k] + nu * (cross_curve(padded) + curve_z[at]) - (
                base[1] * cross_slope(padded) + base[2] * slope_z[at])
            if t:
                section[k] = 0.5 * vx[0, k, 2:rows + 2] + 0.5 * (base[k] + TIME_STEP * rate)
            else:
                section[k] = base[k] + TIME_STEP * rate
            if k == 2:
                flat = wide(section[2])
                edge = dot(sums_a[...], parts(flat))
                zbo[t, 0] = tall(edge[:ra], rows)
                zbo[t, 1] = tall(edge[ra:], rows)
                copies += [
                    send(6, t, zbo.at[t, 0], zb.at[t, 0], 1, 0),
                    send(7, t, zbo.at[t, 1], zb.at[t, 1], -1, 0),
                ]
            if k == 1:
                sx[t, 2:rows + 2] = section[1]
                copies += [
                    send(4, t, sx.at[t, rows:rows + 2], sx.at[t, 0:2], 0, 1),
                    send(5, t, sx.at[t, 2:4], sx.at[t, rows + 2:rows + 4], 0, -1),
                ]
        joined = stream_first(section[0])
        arrive(copies)
        kept += copies
        met = jnp.concatenate([flat, wide(zb[t, 0]), wide(zb[t, 1])], axis=0)
        source = joined + cross_slope(sx[t]) + tall(dot(form_a[:cells], parts(met)), rows)
        cx[t, low:high] = source
        copies = []
        edge = dot(sums_c[...], parts(wide(source)))
        number = 12
        for side in range(2):
            zco[t, side] = tall(edge[side * rc:(side + 1) * rc], rows)
            da = 1 - 2 * side
            copies += [
                send(number, t, zco.at[t, side], zc.at[t, side, low:high], da, 0),
                send(number + 1, t, zco.at[t, side], zc.at[t, side, low - rows:low], da, 1),
                send(number + 2, t, zco.at[t, side], zc.at[t, side, high:high + rows], da, -1),
                send(number + 3, t, zco.at[t, side, rows - 1:rows], zc.at[t, side, 0:1], da, 2),
                send(number + 4, t, zco.at[t, side, 0:1], zc.at[t, side, high + rows:high + rows + 1], da, -2),
            ]
            number += 5
        copies += [
            send(8, t, cx.at[t, low:high], cx.at[t, low - rows:low], 0, 1),
            send(9, t, cx.at[t, low:high], cx.at[t, high:high + rows], 0, -1),
            send(10, t, cx.at[t, high - 1:high], cx.at[t, 0:1], 0, 2),
            send(11, t, cx.at[t, low:low + 1], cx.at[t, high + rows:high + rows + 1], 0, -2),
        ]
        arrive(copies)
        kept += copies
        joint = jnp.concatenate([cx[t], zc[t, 0], zc[t, 1]], axis=1)
        columns = joint.shape[-1]
        joint = parts(wide(joint))
        powers = dot(form_c[:4 * cells], joint)
        t0, t1, t2, t3 = [tall(powers[i * cells:(i + 1) * cells], total) for i in range(4)]
        x = inside(t2[1:total - 1] + beside(t3), 1 - FAR)
        x = inside(t1[2:total - 2] + beside(x), 2 - FAR)
        scalar = inside(t0[3:total - 3] + beside(x), 3 - FAR)
        results = [section[0] + stream_first(scalar[2:rows + 2]), section[1] + cross_slope(scalar)]
        for k in range(2):
            if t:
                deliver(k, results[k])
            else:
                vx[1, k, 2:rows + 2] = results[k]
        if not t:
            started = start(1, 0, 2, 0)
        slopes = dot(form_c[4 * cells:], joint[:, 2 * columns:(total - 2) * columns])
        d0, d1, d2, d3 = [tall(slopes[i * cells:(i + 1) * cells], total - 4) for i in range(4)]
        n = total - 4
        x = inside(d2[1:n - 1] + beside(d3), 3 - FAR)
        x = inside(d1[2:n - 2] + beside(x), 4 - FAR)
        slope = d0[3:n - 3] + beside(x)
        if t:
            deliver(2, section[2] + slope)
        else:
            vx[1, 2, 2:rows + 2] = section[2] + slope
            started = started + start(1, 2, 3, 22)
    for copy, dc in kept:
        there(dc, copy.wait_send)


def solution(mesh):
    spans, crosses = mesh.shape["span"], mesh.shape["cross"]

    def per_device(velocity, viscosity):
        _, cells, rows, columns = velocity.shape
        k1, k2 = symbols(cells * spans)
        g = 1.0 / (4.0 + k2)
        sums_a, form_a = block_form([1j * k1, -k2 + 0j], cells, 8)
        powers = [g ** (m + 1) + 0j for m in range(4)]
        sums_c, form_c = block_form(powers + [1j * k1 * p for p in powers], cells, RANK)
        table = np.concatenate([
            np.pad(part, ((0, 0), (0, form_c.shape[1] - part.shape[1])))
            for part in (sums_a, sums_c, form_a, form_c)
        ])
        table = np.pad(table, ((0, 0), (0, -table.shape[1] % 128)))
        total = rows + 2 * FAR
        f32 = jnp.float32
        hbm = pl.BlockSpec(memory_space=pltpu.HBM)
        vmem = pl.BlockSpec(memory_space=pltpu.VMEM)
        result = pl.pallas_call(
            lambda *refs: kernel(spans, crosses, *refs),
            out_shape=jax.ShapeDtypeStruct((3, cells * rows, columns), f32),
            in_specs=[hbm] * 3,
            out_specs=vmem,
            scratch_shapes=[
                pltpu.VMEM((3, cells * rows, columns), f32),
                pltpu.VMEM((cells * rows, columns), f32),
                pltpu.VMEM(table.shape, f32),
                pltpu.SemaphoreType.DMA((3,)),
                pltpu.VMEM((2, 3, rows + 4, cells, columns), f32),
                pltpu.VMEM((2, 2, 3 * rows, 8, columns), f32),
                pltpu.VMEM((2, 2, 3 * rows, 8, columns), f32),
                pltpu.VMEM((2, rows + 4, cells, columns), f32),
                pltpu.VMEM((2, 2, rows, 8, columns), f32),
                pltpu.VMEM((2, 2, rows, 8, columns), f32),
                pltpu.VMEM((2, total, cells, columns), f32),
                pltpu.VMEM((2, 2, total, RANK, columns), f32),
                pltpu.VMEM((2, 2, rows, RANK, columns), f32),
                pltpu.VMEM((rows, cells, columns), f32),
                pltpu.SemaphoreType.DMA((2, 26)),
                pltpu.SemaphoreType.DMA((2, 26)),
            ],
            compiler_params=pltpu.CompilerParams(
                collective_id=0, has_side_effects=True, vmem_limit_bytes=63 * 1024 * 1024
            ),
        )(
            velocity.reshape(3, cells * rows, columns), viscosity.reshape(cells * rows, columns),
            jnp.asarray(table),
        )
        return result.reshape(3, cells, rows, columns)

    return jax.shard_map(
        per_device,
        mesh=mesh,
        in_specs=(P(None, "span", "cross", None), P("span", "cross", None)),
        out_specs=P(None, "span", "cross", None),
        check_vma=False,
    )
```

```python
import jax
import jax.numpy as jnp
import numpy as np
from jax import lax
from jax.experimental import pallas as pl
from jax.experimental.pallas import tpu as pltpu
from jax.sharding import PartitionSpec as P

MESH = pl.DeviceIdType.MESH
TIME_STEP = 0.1
FAR = 5
RANK = 8


def symbols(length):
    w = 2.0 * np.pi * np.arange(length) / length
    k1 = (14 / 9 * np.sin(w) + 1 / 18 * np.sin(2 * w)) / (1 + 2 / 3 * np.cos(w))
    k2 = (24 / 11 * (1 - np.cos(w)) + 3 / 22 * (1 - np.cos(2 * w))) / (1 + 4 / 11 * np.cos(w))
    return k1, k2


def triple(table):
    high = table.astype(jnp.bfloat16)
    low = (table - high.astype(np.float64)).astype(jnp.bfloat16)
    return np.concatenate([high, low, high], axis=1).astype(np.float32)


def parts(values):
    high = values.astype(jnp.bfloat16)
    low = (values - high.astype(jnp.float32)).astype(jnp.bfloat16)
    return jnp.concatenate([high, high, low], axis=0)


def block_form(table, cells, rank):
    length = table[0].shape[0]
    kernels = [np.fft.ifft(symbol).real for symbol in table]
    offset = np.arange(cells)[:, None] - np.arange(cells)[None, :]
    own = np.concatenate([h[offset % length] for h in kernels])
    left = np.concatenate([h[(offset + cells) % length] for h in kernels])
    right = np.concatenate([h[(offset - cells) % length] for h in kernels])
    to_right = np.linalg.svd(left)[2][:rank]
    to_left = np.linalg.svd(right)[2][:rank]
    sums = np.concatenate([to_right, to_left])
    apply = np.concatenate([own, left @ to_right.T, right @ to_left.T], axis=1)
    return triple(sums), triple(apply)


def turn(values, shift):
    axis = values.ndim - 1
    return pltpu.roll(values, shift % values.shape[axis], axis)


def wide(values):
    return jnp.concatenate([values[i] for i in range(values.shape[0])], axis=-1)


def tall(values, count):
    n = values.shape[-1] // count
    return jnp.stack([values[:, i * n:(i + 1) * n] for i in range(count)])


def stream_pair(values):
    up_one, down_one = turn(values, -1), turn(values, 1)
    up_two, down_two = turn(values, -2), turn(values, 2)
    first = (8.0 * (up_one - down_one) - (up_two - down_two)) * (1.0 / 12.0)
    curve = (16.0 * (up_one + down_one) - (up_two + down_two) - 30.0 * values) * (1.0 / 12.0)
    return first, curve


def stream_first(values):
    return (8.0 * (turn(values, -1) - turn(values, 1)) - (turn(values, -2) - turn(values, 2))) * (1.0 / 12.0)


def cross_slope(p):
    n = p.shape[0]
    return (8.0 * (p[3:n - 1] - p[1:n - 3]) - (p[4:] - p[:n - 4])) * (1.0 / 12.0)


def cross_curve(p):
    n = p.shape[0]
    return (16.0 * (p[3:n - 1] + p[1:n - 3]) - (p[4:] + p[:n - 4]) - 30.0 * p[2:n - 2]) * (1.0 / 12.0)


def beside(p):
    mid = p[1:p.shape[0] - 1]
    return turn(mid, 1) + turn(mid, -1) + p[2:] + p[:p.shape[0] - 2]


def kernel(spans, crosses, vel_hbm, visc_hbm, table_hbm, out, vel, visc, table, load_sem,
           vx, za, zao, sx, zb, zbo, cx, zc, zco, nu_ref, send_sem, recv_sem):
    a, c = lax.axis_index("span"), lax.axis_index("cross")
    rows, cells = nu_ref.shape[0], nu_ref.shape[1]
    ra = rc = RANK
    loads = [
        pltpu.make_async_copy(source, target, load_sem.at[i])
        for i, (source, target) in enumerate([(vel_hbm, vel), (visc_hbm, visc), (table_hbm, table)])
    ]
    for load in loads:
        load.start()
    n_sums = 2 * RANK
    sums_a = table.at[0:n_sums]
    sums_c = table.at[n_sums:2 * n_sums]
    form_a = table.at[2 * n_sums:2 * n_sums + 2 * cells]
    form_c = table.at[2 * n_sums + 2 * cells:]

    def device(da, dc):
        return lax.rem(a + (da + spans), spans), lax.rem(c + (dc + crosses), crosses)

    def there(dc, action):
        if dc == 0:
            action()
        else:
            pl.when((c + dc >= 0) & (c + dc < crosses))(action)

    def clear(dc, refs):
        def action():
            for ref in refs:
                ref[...] = jnp.zeros(ref.shape, ref.dtype)

        pl.when((c + dc < 0) | (c + dc >= crosses))(action)

    barrier = pltpu.get_barrier_semaphore()
    greeted = [(da, dc) for da in (-1, 0, 1) for dc in (-2, -1, 0, 1, 2) if (da, dc) != (0, 0)]
    for da, dc in greeted:
        pl.semaphore_signal(barrier, inc=1, device_id=device(da, dc), device_id_type=MESH)

    def send(number, section, src, dst, da, dc):
        copy = pltpu.make_async_remote_copy(
            src_ref=src, dst_ref=dst, send_sem=send_sem.at[section, number],
            recv_sem=recv_sem.at[section, number], device_id=device(da, dc), device_id_type=MESH,
        )
        there(dc, copy.start)
        return copy, dc

    def arrive(copies):
        for copy, dc in copies:
            there(-dc, copy.wait_recv)

    def inside(values, first):
        kept_rows = []
        for i in range(values.shape[0]):
            number = first + i
            if number < 0:
                kept_rows.append(jnp.where(c * rows + number >= 0, values[i], 0.0))
            elif number >= rows:
                kept_rows.append(jnp.where(c * rows + number < rows * crosses, values[i], 0.0))
            else:
                kept_rows.append(values[i])
        return jnp.stack(kept_rows)

    def dot(left, right):
        rest = jnp.zeros((left.shape[1] - right.shape[0], right.shape[1]), right.dtype)
        right = jnp.concatenate([right, rest], axis=0)
        return jnp.dot(left.astype(jnp.bfloat16), right, preferred_element_type=jnp.float32)

    low, high = FAR, FAR + rows
    total = rows + 2 * FAR
    clear(-1, [vx.at[:, :, 0:2], sx.at[:, 0:2], cx.at[:, low - rows:low], zc.at[:, :, low - rows:low]])
    clear(1, [vx.at[:, :, rows + 2:], sx.at[:, rows + 2:], cx.at[:, high:high + rows], zc.at[:, :, high:high + rows]])
    clear(-2, [cx.at[:, 0:1], zc.at[:, :, 0:1]])
    clear(2, [cx.at[:, total - 1:], zc.at[:, :, total - 1:]])
    for load in loads:
        load.wait()
    for y in range(rows):
        own = pl.ds(y, cells, stride=rows)
        for k in range(3):
            vx[0, k, y + 2] = vel[k, own, :]
        nu_ref[y] = visc[own, :]

    def sums_of(t, first, last):
        ends = slice(first * rows, last * rows)
        values = vx[t, first:last, 2:rows + 2]
        values = values.reshape((last - first) * rows, cells, values.shape[-1])
        edge = dot(sums_a[...], parts(wide(values)))
        zao[t, 0, ends] = tall(edge[:ra], values.shape[0])
        zao[t, 1, ends] = tall(edge[ra:], values.shape[0])

    def start(t, first, last, number):
        ends = slice(first * rows, last * rows)
        sent = [
            send(number, t, vx.at[t, first:last, rows:rows + 2], vx.at[t, first:last, 0:2], 0, 1),
            send(number + 1, t, vx.at[t, first:last, 2:4], vx.at[t, first:last, rows + 2:rows + 4], 0, -1),
        ]
        if t:
            sums_of(t, first, last)
        sent += [
            send(number + 2, t, zao.at[t, 0, ends], za.at[t, 0, ends], 1, 0),
            send(number + 3, t, zao.at[t, 1, ends], za.at[t, 1, ends], -1, 0),
        ]
        return sent

    def deliver(k, result):
        for y in range(rows):
            out[k, pl.ds(y, cells, stride=rows), :] = result[y]

    kept = []
    for t in range(2):
        if not t:
            sums_of(0, 0, 3)
            pl.semaphore_wait(barrier, len(greeted))
            started = start(0, 0, 3, 0)
        copies = started
        base = vx[t, :, 2:rows + 2]
        flat = wide(base.reshape(3 * rows, cells, base.shape[-1]))
        slope_x, curve_x = stream_pair(base.reshape(3 * rows, cells, base.shape[-1]))
        nu = nu_ref[...]
        early = [
            nu * curve_x[k * rows:(k + 1) * rows] - base[0] * slope_x[k * rows:(k + 1) * rows]
            for k in range(3)
        ]
        arrive(copies)
        kept += copies
        met = jnp.concatenate([flat, wide(za[t, 0]), wide(za[t, 1])], axis=0)
        pair = dot(form_a[...], parts(met))
        slope_z = tall(pair[:cells], 3 * rows)
        curve_z = tall(pair[cells:], 3 * rows)
        section = [None] * 3
        copies = []
        for k in (2, 1, 0):
            padded = vx[t, k]
            at = slice(k * rows, (k + 1) * rows)
            rate = early[k] + nu * (cross_curve(padded) + curve_z[at]) - (
                base[1] * cross_slope(padded) + base[2] * slope_z[at])
            if t:
                section[k] = 0.5 * vx[0, k, 2:rows + 2] + 0.5 * (base[k] + TIME_STEP * rate)
            else:
                section[k] = base[k] + TIME_STEP * rate
            if k == 2:
                flat = wide(section[2])
                edge = dot(sums_a[...], parts(flat))
                zbo[t, 0] = tall(edge[:ra], rows)
                zbo[t, 1] = tall(edge[ra:], rows)
                copies += [
                    send(6, t, zbo.at[t, 0], zb.at[t, 0], 1, 0),
                    send(7, t, zbo.at[t, 1], zb.at[t, 1], -1, 0),
                ]
            if k == 1:
                sx[t, 2:rows + 2] = section[1]
                copies += [
                    send(4, t, sx.at[t, rows:rows + 2], sx.at[t, 0:2], 0, 1),
                    send(5, t, sx.at[t, 2:4], sx.at[t, rows + 2:rows + 4], 0, -1),
                ]
        joined = stream_first(section[0])
        arrive(copies)
        kept += copies
        met = jnp.concatenate([flat, wide(zb[t, 0]), wide(zb[t, 1])], axis=0)
        source = joined + cross_slope(sx[t]) + tall(dot(form_a[:cells], parts(met)), rows)
        cx[t, low:high] = source
        copies = [
            send(8, t, cx.at[t, low:high], cx.at[t, low - rows:low], 0, 1),
            send(9, t, cx.at[t, low:high], cx.at[t, high:high + rows], 0, -1),
            send(10, t, cx.at[t, high - 1:high], cx.at[t, 0:1], 0, 2),
            send(11, t, cx.at[t, low:low + 1], cx.at[t, high + rows:high + rows + 1], 0, -2),
        ]
        edge = dot(sums_c[...], parts(wide(source)))
        number = 12
        for side in range(2):
            zco[t, side] = tall(edge[side * rc:(side + 1) * rc], rows)
            da = 1 - 2 * side
            copies += [
                send(number, t, zco.at[t, side], zc.at[t, side, low:high], da, 0),
                send(number + 1, t, zco.at[t, side], zc.at[t, side, low - rows:low], da, 1),
                send(number + 2, t, zco.at[t, side], zc.at[t, side, high:high + rows], da, -1),
                send(number + 3, t, zco.at[t, side, rows - 1:rows], zc.at[t, side, 0:1], da, 2),
                send(number + 4, t, zco.at[t, side, 0:1], zc.at[t, side, high + rows:high + rows + 1], da, -2),
            ]
            number += 5
        arrive(copies)
        kept += copies
        joint = jnp.concatenate([cx[t], zc[t, 0], zc[t, 1]], axis=1)
        columns = joint.shape[-1]
        joint = parts(wide(joint))
        powers = dot(form_c[:4 * cells], joint)
        t0, t1, t2, t3 = [tall(powers[i * cells:(i + 1) * cells], total) for i in range(4)]
        x = inside(t2[1:total - 1] + beside(t3), 1 - FAR)
        x = inside(t1[2:total - 2] + beside(x), 2 - FAR)
        scalar = inside(t0[3:total - 3] + beside(x), 3 - FAR)
        results = [section[0] + stream_first(scalar[2:rows + 2]), section[1] + cross_slope(scalar)]
        for k in range(2):
            if t:
                deliver(k, results[k])
            else:
                vx[1, k, 2:rows + 2] = results[k]
        if not t:
            started = start(1, 0, 2, 0)
        slopes = dot(form_c[4 * cells:], joint[:, 2 * columns:(total - 2) * columns])
        d0, d1, d2, d3 = [tall(slopes[i * cells:(i + 1) * cells], total - 4) for i in range(4)]
        n = total - 4
        x = inside(d2[1:n - 1] + beside(d3), 3 - FAR)
        x = inside(d1[2:n - 2] + beside(x), 4 - FAR)
        slope = d0[3:n - 3] + beside(x)
        if t:
            deliver(2, section[2] + slope)
        else:
            vx[1, 2, 2:rows + 2] = section[2] + slope
            started = started + start(1, 2, 3, 22)
    for copy, dc in kept:
        there(dc, copy.wait_send)


def solution(mesh):
    spans, crosses = mesh.shape["span"], mesh.shape["cross"]

    def per_device(velocity, viscosity):
        _, cells, rows, columns = velocity.shape
        k1, k2 = symbols(cells * spans)
        g = 1.0 / (4.0 + k2)
        sums_a, form_a = block_form([1j * k1, -k2 + 0j], cells, 8)
        powers = [g ** (m + 1) + 0j for m in range(4)]
        sums_c, form_c = block_form(powers + [1j * k1 * p for p in powers], cells, RANK)
        table = np.concatenate([
            np.pad(part, ((0, 0), (0, form_c.shape[1] - part.shape[1])))
            for part in (sums_a, sums_c, form_a, form_c)
        ])
        table = np.pad(table, ((0, 0), (0, -table.shape[1] % 128)))
        total = rows + 2 * FAR
        f32 = jnp.float32
        hbm = pl.BlockSpec(memory_space=pltpu.HBM)
        vmem = pl.BlockSpec(memory_space=pltpu.VMEM)
        result = pl.pallas_call(
            lambda *refs: kernel(spans, crosses, *refs),
            out_shape=jax.ShapeDtypeStruct((3, cells * rows, columns), f32),
            in_specs=[hbm] * 3,
            out_specs=vmem,
            scratch_shapes=[
                pltpu.VMEM((3, cells * rows, columns), f32),
                pltpu.VMEM((cells * rows, columns), f32),
                pltpu.VMEM(table.shape, f32),
                pltpu.SemaphoreType.DMA((3,)),
                pltpu.VMEM((2, 3, rows + 4, cells, columns), f32),
                pltpu.VMEM((2, 2, 3 * rows, 8, columns), f32),
                pltpu.VMEM((2, 2, 3 * rows, 8, columns), f32),
                pltpu.VMEM((2, rows + 4, cells, columns), f32),
                pltpu.VMEM((2, 2, rows, 8, columns), f32),
                pltpu.VMEM((2, 2, rows, 8, columns), f32),
                pltpu.VMEM((2, total, cells, columns), f32),
                pltpu.VMEM((2, 2, total, RANK, columns), f32),
                pltpu.VMEM((2, 2, rows, RANK, columns), f32),
                pltpu.VMEM((rows, cells, columns), f32),
                pltpu.SemaphoreType.DMA((2, 26)),
                pltpu.SemaphoreType.DMA((2, 26)),
            ],
            compiler_params=pltpu.CompilerParams(
                collective_id=0, has_side_effects=True, vmem_limit_bytes=63 * 1024 * 1024
            ),
        )(
            velocity.reshape(3, cells * rows, columns), viscosity.reshape(cells * rows, columns),
            jnp.asarray(table),
        )
        return result.reshape(3, cells, rows, columns)

    return jax.shard_map(
        per_device,
        mesh=mesh,
        in_specs=(P(None, "span", "cross", None), P("span", "cross", None)),
        out_specs=P(None, "span", "cross", None),
        check_vma=False,
    )
```
